128 devices in a mesh: pages: 32 (over y, x, core), rep: 4 (over z).
Axes of the slice: x: 4, y: 4, z: 4, core: 2. Of those that a mesh axis runs over, the one named last changes fastest.
Arguments:
- features: bfloat16 [1280, 256, 1152], P('pages'), may hold values from -6 to 6
- queries: bfloat16 [512, 32, 128], P(('pages', 'rep')), may hold values from -6 to 6
- proj_weight: bfloat16 [1152, 128], replicated, may hold values from -0.1875 to 0.1875
- page_ids: int32 [512, 16], P(('pages', 'rep')), may hold values from 0 to 1279, as said below
Outputs:
- scores: float32 [512, 16], P(('pages', 'rep'))
- grad_query: float32 [512, 32, 128], P(('pages', 'rep'))
- grad_proj: float32 [1152, 128], replicated
The draws below stay inside these ranges and needn't reach their ends.
Inputs may be any that keep to these rules, and one draw needn't show every extreme that they name: `page_ids`: page ids k * 40 to (k + 1) * 40 - 1 form owner range k. Among the 64 entries of the queries of one device (an aligned block of 4 queries), at most 8 fall in one owner range; in every draw some owner ranges receive exactly 8 from every such block.
All inputs are finite; a program needn't handle non-finite values.
Results may differ from the reference program's by a relative error of at most 0.0045.
The reference program's roundings to bfloat16 on the way (of `page_emb`, `query_emb`, `sim_grad` and `projected_grad`) count: a program that leaves them out, or rounds other values in their place, can miss the bound.
Values may be sent and summed in bfloat16 or wider, within the bound.
No kernel may reach another device: no remote copies, remote signals or barrier semaphores. Data moves between devices by JAX's collectives and lax.ppermute only.
A program may use at most 256 MiB of HBM per device.

```python
import jax
import jax.numpy as jnp
from jax import lax

D_FEAT = 1152
PROJ = 128
QTOK = 32
TOKP = 256
P_DEV = 40
Q_DEV = 4
LIST = 16
PAGES = 1280
QUERIES = 512
N_REP = 4


hot_count = 4


def draw_page_ids(key, part):
    key = jax.random.fold_in(key, 7)
    owners = PAGES // P_DEV
    blocks = QUERIES // Q_DEV
    pair_count = Q_DEV * LIST
    capacity = 2 * Q_DEV
    hot_key, start_key, order_key, slot_key = jax.random.split(key, 4)
    hot_base = jax.random.randint(hot_key, (), 0, owners)
    index = jnp.arange(pair_count, dtype=jnp.int32)
    hot_part = index < hot_count * capacity
    hot_owner = (hot_base + index // capacity) % owners
    starts = jax.random.randint(start_key, (blocks, 1), 0, owners - hot_count)
    remain = index - hot_count * capacity
    cold_owner = (hot_base + hot_count + (starts + remain[None, :]) % (owners - hot_count)) % owners
    owner_of = jnp.where(hot_part[None, :], hot_owner[None, :], cold_owner)
    orders = jax.vmap(lambda sub: jax.random.permutation(sub, pair_count))(jax.random.split(order_key, blocks))
    owner_of = jnp.take_along_axis(owner_of, orders, axis=1)
    local_page = jax.random.randint(slot_key, (blocks, pair_count), 0, P_DEV)
    return (owner_of * P_DEV + local_page).reshape(QUERIES, LIST).astype(jnp.int32)


def shard_levels(key, shape, pieces, smallest, high):
    def one(axis_at, shards_of):
        draws = jax.random.uniform(jax.random.fold_in(jax.random.fold_in(key, 6), axis_at), (shards_of,), jnp.float32, smallest / len(pieces), high / len(pieces))
        return jnp.repeat(jnp.exp(draws), shape[axis_at] // shards_of).reshape((-1,) + (1,) * (len(shape) - axis_at - 1))

    gain = one(*pieces[0])
    for cut in pieces[1:]:
        gain = gain * one(*cut)
    return gain


def bell_draw(stream_key, dims, width, reach, pieces=(), kind=jnp.bfloat16):
    factor_of = shard_levels(stream_key, dims, pieces, -0.22, 0.18) if pieces else 1.0
    array = jax.random.normal(stream_key, dims, jnp.float32) * width * factor_of
    return jnp.minimum(jnp.maximum(array, -reach), reach).astype(kind)


def setup_inputs(seed: int = 0) -> dict:
    splits = jax.random.split(jax.random.key(seed), 5)
    features = bell_draw(splits[0], (PAGES, TOKP, D_FEAT), 1.0, 6.0, ((0, 32),))
    queries = bell_draw(splits[1], (QUERIES, QTOK, PROJ), 1.0, 6.0, ((0, 128),))
    proj_weight = bell_draw(splits[2], (D_FEAT, PROJ), D_FEAT ** -0.5, 0.1875)
    page_ids = draw_page_ids(jax.random.fold_in(splits[4], 71), 0)
    return {"features": features, "queries": queries, "proj_weight": proj_weight, "page_ids": page_ids}


epsilon = 1e-06
smoothing = 0.05

def unit_backward(values, scale, upstream):
    inner = lax.optimization_barrier(jnp.sum(values * upstream, axis=-1, keepdims=True))
    return upstream * scale - values * scale ** 3 * inner

def reference(features, queries, proj_weight, page_ids):
    rows = features.reshape(PAGES * TOKP, D_FEAT)
    projected = jnp.dot(rows, proj_weight, preferred_element_type=jnp.float32)
    page_scale = lax.rsqrt(lax.optimization_barrier(jnp.sum(projected * projected, axis=1, keepdims=True)) + epsilon)
    page_emb = (projected * page_scale).astype(jnp.bfloat16).reshape(PAGES, TOKP, PROJ)
    query_wide = queries.astype(jnp.float32)
    query_scale = lax.rsqrt(lax.optimization_barrier(jnp.sum(query_wide * query_wide, axis=2, keepdims=True)) + epsilon)
    query_emb = (query_wide * query_scale).astype(jnp.bfloat16)

    def forward(item):
        query_one, listed_ids = item
        chosen = page_emb[listed_ids].astype(jnp.float32)
        sims = jnp.einsum('tf,kjf->ktj', query_one.astype(jnp.float32), chosen)
        totals = lax.optimization_barrier(jnp.sum(jnp.exp(sims / smoothing), axis=2))
        return lax.optimization_barrier(jnp.sum(smoothing * jnp.log(totals), axis=1))
    scores = lax.map(forward, (query_emb, page_ids))
    exp_scores = jnp.exp(scores)
    probability = exp_scores / lax.optimization_barrier(jnp.sum(exp_scores, axis=1, keepdims=True))
    score_grad = probability - (jnp.arange(LIST) == 0).astype(jnp.float32)[None, :]
    group = (jnp.arange(QUERIES) // Q_DEV % N_REP).astype(jnp.int32)

    def backward(carry, item):
        query_one, listed_ids, weight_row, group_one = item
        chosen = page_emb[listed_ids]
        sims = jnp.einsum('tf,kjf->ktj', query_one.astype(jnp.float32), chosen.astype(jnp.float32))
        expw = jnp.exp(sims / smoothing)
        totals = lax.optimization_barrier(jnp.sum(expw, axis=2, keepdims=True))
        sim_grad = (weight_row[:, None, None] * (expw / totals)).astype(jnp.bfloat16)
        query_grad = jnp.einsum('ktj,kjf->tf', sim_grad.astype(jnp.float32), chosen.astype(jnp.float32))
        page_grad = jnp.einsum('ktj,tf->kjf', sim_grad.astype(jnp.float32), query_one.astype(jnp.float32))
        carry = carry.at[group_one, listed_ids].add(page_grad)
        return (carry, query_grad)
    init = jnp.zeros((N_REP, PAGES, TOKP, PROJ), jnp.float32)
    page_unit_grad, query_unit_grad = lax.scan(backward, init, (query_emb, page_ids, score_grad, group))
    grad_query = unit_backward(query_wide, query_scale, query_unit_grad)
    grad_proj = jnp.zeros((D_FEAT, PROJ), jnp.float32)
    for group_index in range(N_REP):
        upstream = page_unit_grad[group_index].reshape(PAGES * TOKP, PROJ)
        projected_grad = unit_backward(projected, page_scale, upstream).astype(jnp.bfloat16)
        grad_proj = grad_proj + jnp.dot(rows.T, projected_grad, preferred_element_type=jnp.float32)
    return (scores, grad_query, grad_proj)
```

```python
import math

import jax
import jax.numpy as jnp
from jax import lax
from jax.experimental import pallas as pl
from jax.experimental.pallas import tpu as pltpu
from jax.sharding import PartitionSpec as P

epsilon = 1e-06
smoothing = 0.05
exp2_factor = 1.0 / (smoothing * math.log(2.0))
log2_factor = smoothing * math.log(2.0)

f32 = jnp.float32
bf16 = jnp.bfloat16
i32 = jnp.int32

OWNERS = 32
SLOTS = 8
ENTRIES = OWNERS * SLOTS
QBLOCK = 4
LISTED = 16
QTOK = 32
TOKP = 256
PROJ = 128
P_DEV = 40
D_FEAT = 1152
META = 16
QROWS = QBLOCK * QTOK
QSTRIDE = QROWS + META
CHUNK = 8
LANES = CHUNK * QTOK
MAX_CHUNKS = 72
POSITIONS = 640
MIB = 1 << 20


def iota(shape, dim):
    return lax.broadcasted_iota(i32, shape, dim)


def row_to_col(row, n):
    same = iota((n, n), 0) == iota((n, n), 1)
    return jnp.sum(jnp.where(same, jnp.broadcast_to(row, (n, n)), 0.0), axis=1, keepdims=True)


def col_to_row(col, n):
    same = iota((n, n), 0) == iota((n, n), 1)
    return jnp.sum(jnp.where(same, jnp.broadcast_to(col, (n, n)), 0.0), axis=0, keepdims=True)


def contract_first(a, b):
    return lax.dot_general(a, b, (((0,), (0,)), ((), ())), preferred_element_type=f32)


def contract_last(a, b):
    return lax.dot_general(a, b, (((1,), (1,)), ((), ())), preferred_element_type=f32)


def send_kernel(ids_ref, q_ref, out_ref):
    wide = q_ref[...].reshape(QROWS, PROJ).astype(f32)
    scale = lax.rsqrt(jnp.sum(wide * wide, axis=1, keepdims=True) + epsilon)
    emb = (wide * scale).astype(bf16)
    out_ref[:, 0:QROWS, :] = jnp.broadcast_to(emb[None], (OWNERS, QROWS, PROJ))
    ids = ids_ref[...].astype(f32)
    owner = jnp.floor((ids + 0.5) * (1.0 / P_DEV))
    local = ids - owner * P_DEV
    owner_col = jnp.concatenate([row_to_col(owner[q : q + 1], LISTED) for q in range(QBLOCK)], 0)
    local_col = jnp.concatenate([row_to_col(local[q : q + 1], LISTED) for q in range(QBLOCK)], 0)
    pairs = QBLOCK * LISTED
    lane = iota((pairs, 128), 1)
    entry = iota((pairs, 128), 0)
    hit = (owner_col.astype(i32) == lane).astype(f32)
    before = (iota((pairs, pairs), 1) < iota((pairs, pairs), 0)).astype(f32)
    rank = jnp.sum(
        hit * jnp.dot(before, hit, preferred_element_type=f32), axis=1, keepdims=True
    ).astype(i32)
    code = (entry // LISTED) * 2 + (entry % LISTED == 0).astype(i32)
    value = jnp.where(
        rank == lane,
        local_col + 1.0,
        jnp.where(rank + SLOTS == lane, code.astype(f32), 0.0),
    )
    value = jnp.where(lane < 2 * SLOTS, value, 0.0)
    meta = contract_first(hit, value)[0:OWNERS]
    out_ref[:, QROWS:QSTRIDE, :] = jnp.broadcast_to(
        meta[:, None, :], (OWNERS, META, PROJ)
    ).astype(bf16)


def send_queries(page_ids, queries):
    return pl.pallas_call(
        send_kernel,
        out_shape=jax.ShapeDtypeStruct((OWNERS, QSTRIDE, PROJ), bf16),
        name="send_queries",
    )(page_ids, queries)


def project_kernel(x_ref, w_ref, proj_ref, emb_ref):
    value = jnp.dot(x_ref[...], w_ref[...], preferred_element_type=f32)
    proj_ref[...] = value
    scale = lax.rsqrt(jnp.sum(value * value, axis=1, keepdims=True) + epsilon)
    emb_ref[...] = (value * scale).astype(bf16)


def project(rows, weight):
    total = rows.shape[0]
    block = 512
    return pl.pallas_call(
        project_kernel,
        grid=(total // block,),
        in_specs=[
            pl.BlockSpec((block, D_FEAT), lambda i: (i, 0)),
            pl.BlockSpec((D_FEAT, PROJ), lambda i: (0, 0)),
        ],
        out_specs=[
            pl.BlockSpec((block, PROJ), lambda i: (i, 0)),
            pl.BlockSpec((block, PROJ), lambda i: (i, 0)),
        ],
        out_shape=[
            jax.ShapeDtypeStruct((total, PROJ), f32),
            jax.ShapeDtypeStruct((total, PROJ), bf16),
        ],
        compiler_params=pltpu.CompilerParams(vmem_limit_bytes=32 * MIB),
        cost_estimate=pl.CostEstimate(
            flops=2 * total * D_FEAT * PROJ,
            bytes_accessed=total * (2 * D_FEAT + 6 * PROJ),
            transcendentals=0,
        ),
        name="project",
    )(rows, weight)


def slot_columns(recv_ref):
    meta = recv_ref[...].reshape(OWNERS, QSTRIDE, PROJ)[:, QROWS:QSTRIDE, :].astype(f32)
    meta = meta[:, 0:SLOTS, :].reshape(ENTRIES, PROJ)
    lane = iota((ENTRIES, PROJ), 1)
    slot = iota((ENTRIES, PROJ), 0) % SLOTS
    page = jnp.sum(jnp.where(lane == slot, meta, 0.0), axis=1, keepdims=True).astype(i32) - 1
    code = jnp.sum(jnp.where(lane == slot + SLOTS, meta, 0.0), axis=1, keepdims=True).astype(i32)
    query = (iota((ENTRIES, 1), 0) // SLOTS) * QBLOCK + code // 2
    return page, query, code % 2


def plan_entries(page, query):
    valid = page >= 0
    page_f = page.astype(f32)
    page_row = col_to_row(page_f, ENTRIES)
    earlier = iota((ENTRIES, ENTRIES), 1) < iota((ENTRIES, ENTRIES), 0)
    rank = jnp.sum(
        jnp.where((page_f == page_row) & earlier, 1.0, 0.0), axis=1, keepdims=True
    )
    lane = iota((ENTRIES, 128), 1)
    on_page = (page == lane).astype(f32)
    count = jnp.sum(on_page, axis=0, keepdims=True)
    chunks = jnp.floor((count + (CHUNK - 1)) * (1.0 / CHUNK))
    upper = (iota((128, 128), 0) < iota((128, 128), 1)).astype(f32)
    start = jnp.dot(jnp.broadcast_to(chunks, (8, 128)), upper, preferred_element_type=f32)[0:1]
    position = jnp.sum(on_page * start, axis=1, keepdims=True) * CHUNK + rank
    position = jnp.where(valid, position, -1.0).astype(i32)
    at = position == iota((ENTRIES, POSITIONS), 1)
    entry_id = iota((ENTRIES, 1), 0)
    slot_row = jnp.sum(jnp.where(at, entry_id - ENTRIES, 0), axis=0, keepdims=True) + ENTRIES
    row_of = (query // QBLOCK) * QSTRIDE + (query % QBLOCK) * QTOK
    row_row = jnp.sum(jnp.where(at, row_of, 0), axis=0, keepdims=True)
    query_row = jnp.sum(jnp.where(at, query * QTOK, 0), axis=0, keepdims=True)
    start_col = row_to_col(start, 128)[0:P_DEV]
    chunk_page = (
        jnp.sum(
            jnp.where(start_col <= iota((P_DEV, 128), 1).astype(f32), 1, 0), axis=0, keepdims=True
        )
        - 1
    ) * TOKP
    total = jnp.sum(chunks, axis=1, keepdims=True).astype(i32)
    pad = jnp.zeros((1, POSITIONS - 256), i32)
    last = jnp.concatenate(
        [chunk_page, jnp.broadcast_to(total, (1, 128)), pad], axis=1
    )
    return jnp.concatenate(
        [slot_row, row_row, query_row, last, jnp.zeros((4, POSITIONS), i32)], axis=0
    )


def load_queries(recv_ref, table_ref, chunk):
    parts = []
    for j in range(CHUNK):
        row = pl.multiple_of(table_ref[1, chunk * CHUNK + j], 16)
        parts.append(recv_ref[pl.ds(row, QTOK), :])
    return jnp.concatenate(parts, axis=0)


def load_page(emb_ref, table_ref, chunk):
    return emb_ref[pl.ds(pl.multiple_of(table_ref[3, chunk], TOKP), TOKP), :]


def forward_kernel(recv_ref, emb_ref, back_ref, table_out, logs_ref, exps_ref, table_ref, logs_of, sem):
    page, query, positive = slot_columns(recv_ref)
    table_out[...] = plan_entries(page, query)
    copy = pltpu.make_async_copy(table_out, table_ref, sem)
    copy.start()
    copy.wait()
    group = iota((1, 128), 1) // QTOK

    def pair(step, carry):
        for u in range(2):
            chunk = 2 * step + u
            sims = contract_last(
                load_page(emb_ref, table_ref, chunk), load_queries(recv_ref, table_ref, chunk)
            )
            logs = jnp.log2(jnp.sum(jnp.exp2(sims * exp2_factor), axis=0, keepdims=True))
            logs_ref[pl.ds(chunk, 1), :] = logs
            for j in range(CHUNK):
                tile = logs[:, (j // 4) * 128 : (j // 4) * 128 + 128]
                slot = table_ref[0, chunk * CHUNK + j]
                logs_of[pl.ds(slot, 1), :] = jnp.where(group == j % 4, tile, 0.0)
        return carry

    lax.fori_loop(0, (table_ref[3, 128] + 1) // 2, pair, 0)
    scores = log2_factor * jnp.sum(logs_of[0:ENTRIES, :], axis=1, keepdims=True)
    valid = page >= 0
    exps = jnp.where(valid, jnp.exp(scores), 0.0)
    exps_ref[...] = jnp.broadcast_to(exps, (ENTRIES, 128))
    lane = iota((ENTRIES, 128), 1)
    sums = jnp.sum(jnp.where(query == lane, exps, 0.0), axis=0, keepdims=True)
    slot = iota((ENTRIES, 128), 0) % SLOTS
    spread = jnp.where((lane == slot) & valid, scores, 0.0).reshape(OWNERS, SLOTS, 128)
    spread = jnp.sum(spread, axis=1, keepdims=True)
    which = iota((OWNERS, SLOTS, 128), 1)
    back_ref[...] = jnp.where(
        which == 0, sums[None], jnp.where(which == 1, spread, 0.0)
    )


def forward(recv, emb):
    return pl.pallas_call(
        forward_kernel,
        out_shape=[
            jax.ShapeDtypeStruct((OWNERS, SLOTS, 128), f32),
            jax.ShapeDtypeStruct((8, POSITIONS), i32),
            jax.ShapeDtypeStruct((MAX_CHUNKS, LANES), f32),
            jax.ShapeDtypeStruct((ENTRIES, 128), f32),
        ],
        scratch_shapes=[
            pltpu.SMEM((8, POSITIONS), i32),
            pltpu.VMEM((ENTRIES + 8, 128), f32),
            pltpu.SemaphoreType.DMA,
        ],
        compiler_params=pltpu.CompilerParams(vmem_limit_bytes=32 * MIB),
        name="forward",
    )(recv, emb)


FEAT_PAGES = 4
FEAT_ROWS = FEAT_PAGES * TOKP
FEAT_STEPS = P_DEV // FEAT_PAGES


def backward_kernel(
    table_ref, recv_ref, emb_ref, logs_ref, exps_ref, sums_ref, proj_hbm, feat_hbm,
    query_out, grad_out, weight_of, page_acc, query_acc, proj_ref, feat_ref, sems,
):
    def feature_copy(step):
        part = pl.ds(step * FEAT_ROWS, FEAT_ROWS)
        return pltpu.make_async_copy(feat_hbm.at[part], feat_ref.at[part], sems.at[step])

    proj_copy = pltpu.make_async_copy(proj_hbm, proj_ref, sems.at[FEAT_STEPS])
    proj_copy.start()
    for step in range(FEAT_STEPS):
        feature_copy(step).start()

    page, query, positive = slot_columns(recv_ref)
    sums = jnp.sum(sums_ref[...], axis=0)[0:1]
    lane = iota((ENTRIES, 128), 1)
    total = jnp.sum(jnp.where(query == lane, sums, 0.0), axis=1, keepdims=True)
    valid = page >= 0
    total = jnp.where(valid, total, 1.0)
    weight_of[0:ENTRIES, :] = jnp.where(
        valid, exps_ref[...] / total - positive.astype(f32), 0.0
    )
    weight_of[ENTRIES : ENTRIES + 8, :] = jnp.zeros((8, 128), f32)
    page_acc[...] = jnp.zeros(page_acc.shape, f32)
    query_acc[...] = jnp.zeros(query_acc.shape, f32)
    group = iota((1, 128), 1) // QTOK

    def pair(step, carry):
        results = []
        for u in range(2):
            chunk = 2 * step + u
            tokens = load_page(emb_ref, table_ref, chunk)
            queries = load_queries(recv_ref, table_ref, chunk)
            weights = []
            for half in range(CHUNK // 4):
                tile = jnp.zeros((1, 128), f32)
                for j in range(4):
                    slot = table_ref[0, chunk * CHUNK + half * 4 + j]
                    tile = jnp.where(group == j, weight_of[pl.ds(slot, 1), :], tile)
                weights.append(tile)
            weights = jnp.concatenate(weights, axis=1)
            sims = contract_last(tokens, queries)
            share = jnp.exp2(sims * exp2_factor - logs_ref[pl.ds(chunk, 1), :])
            sim_grad = (share * weights).astype(bf16)
            page_part = jnp.dot(sim_grad, queries, preferred_element_type=f32)
            query_part = contract_first(sim_grad, tokens)
            results.append((chunk, page_part, query_part))
        for chunk, page_part, query_part in results:
            rows = pl.ds(pl.multiple_of(table_ref[3, chunk], TOKP), TOKP)
            page_acc[rows, :] += page_part
            for j in range(CHUNK):
                at = pl.ds(pl.multiple_of(table_ref[2, chunk * CHUNK + j], QTOK), QTOK)
                query_acc[at, :] += query_part[j * QTOK : (j + 1) * QTOK]
        return carry

    lax.fori_loop(0, (table_ref[3, 128] + 1) // 2, pair, 0)
    query_out[...] = query_acc[...].astype(query_out.dtype)
    proj_copy.wait()
    grad_out[...] = jnp.zeros(grad_out.shape, f32)

    def feature_step(step, carry):
        part = pl.ds(pl.multiple_of(step * FEAT_ROWS, FEAT_ROWS), FEAT_ROWS)
        value = proj_ref[part, :]
        upstream = page_acc[part, :]
        scale = lax.rsqrt(jnp.sum(value * value, axis=1, keepdims=True) + epsilon)
        inner = jnp.sum(value * upstream, axis=1, keepdims=True)
        grad = (upstream * scale - value * (scale * scale * scale * inner)).astype(bf16)
        feature_copy(step).wait()
        grad_out[...] += contract_first(feat_ref[part, :], grad)
        return carry

    lax.fori_loop(0, FEAT_STEPS, feature_step, 0)


def backward(table, recv, emb, logs, exps, sums, proj, rows):
    vmem = pl.BlockSpec(memory_space=pltpu.VMEM)
    hbm = pl.BlockSpec(memory_space=pl.ANY)
    return pl.pallas_call(
        backward_kernel,
        in_specs=[pl.BlockSpec(memory_space=pltpu.SMEM), vmem, vmem, vmem, vmem, vmem, hbm, hbm],
        out_specs=[vmem, vmem],
        out_shape=[
            jax.ShapeDtypeStruct((OWNERS * QROWS, PROJ), bf16),
            jax.ShapeDtypeStruct((D_FEAT, PROJ), f32),
        ],
        scratch_shapes=[
            pltpu.VMEM((ENTRIES + 8, 128), f32),
            pltpu.VMEM((P_DEV * TOKP, PROJ), f32),
            pltpu.VMEM((OWNERS * QROWS, PROJ), f32),
            pltpu.VMEM((P_DEV * TOKP, PROJ), f32),
            pltpu.VMEM((P_DEV * TOKP, D_FEAT), bf16),
            pltpu.SemaphoreType.DMA((FEAT_STEPS + 1,)),
        ],
        compiler_params=pltpu.CompilerParams(vmem_limit_bytes=60 * MIB),
        name="backward",
    )(table, recv, emb, logs, exps, sums, proj, rows)


def query_kernel(parts_ref, q_ref, out_ref):
    upstream = jnp.sum(parts_ref[...].astype(f32), axis=0)
    wide = q_ref[...].reshape(QROWS, PROJ).astype(f32)
    scale = lax.rsqrt(jnp.sum(wide * wide, axis=1, keepdims=True) + epsilon)
    inner = jnp.sum(wide * upstream, axis=1, keepdims=True)
    out_ref[...] = (upstream * scale - wide * (scale * scale * scale * inner)).reshape(
        out_ref.shape
    )


def query_grads(parts, queries):
    return pl.pallas_call(
        query_kernel,
        out_shape=jax.ShapeDtypeStruct(queries.shape, f32),
        compiler_params=pltpu.CompilerParams(vmem_limit_bytes=32 * MIB),
        name="query_grads",
    )(parts, queries)


def listed_scores(sums, page_ids):
    owner_of = page_ids.reshape(-1) // P_DEV
    hits = (owner_of[:, None] == jnp.arange(OWNERS, dtype=i32)[None, :]).astype(i32)
    rank_of = jnp.sum(jnp.cumsum(hits, axis=0) * hits, axis=1) - 1
    slots = sums[:, 1, 0:SLOTS]
    pick = (hits != 0)[:, :, None] & (rank_of[:, None] == jnp.arange(SLOTS, dtype=i32))[:, None, :]
    return jnp.sum(jnp.where(pick, slots[None], 0.0), axis=(1, 2)).reshape(page_ids.shape)


def exchange(values, axes):
    return lax.all_to_all(values, axes, split_axis=0, concat_axis=0, tiled=True)


def per_device(features, queries, proj_weight, page_ids):
    everyone = ("pages", "rep")
    devices = lax.axis_size(everyone)
    rows = features.reshape(P_DEV * TOKP, D_FEAT)
    recv = exchange(send_queries(page_ids, queries), "pages").reshape(OWNERS * QSTRIDE, PROJ)
    proj, emb = project(rows, proj_weight)
    back, table, logs, exps = forward(recv, emb)
    sums = exchange(back, "pages")
    query_parts, local_term = backward(table, recv, emb, logs, exps, sums, proj, rows)
    parts = exchange(query_parts.reshape(OWNERS, QROWS, PROJ), "pages")
    grad_query = query_grads(parts, queries)
    scores = listed_scores(sums, page_ids)
    shares = exchange(local_term.astype(bf16).reshape(devices, D_FEAT // devices, PROJ), everyone)
    share = jnp.sum(shares.astype(f32), axis=0).astype(bf16)
    whole = exchange(jnp.broadcast_to(share[None], shares.shape), everyone)
    grad_proj = whole.reshape(D_FEAT, PROJ).astype(f32)
    return (scores, grad_query, grad_proj)


def solution(mesh):
    in_specs = (
        P("pages", None, None),
        P(("pages", "rep"), None, None),
        P(),
        P(("pages", "rep"), None),
    )
    out_specs = (P(("pages", "rep"), None), P(("pages", "rep"), None, None), P())
    return jax.shard_map(
        per_device, mesh=mesh, in_specs=in_specs, out_specs=out_specs, check_vma=False
    )
```

```python
import math

import jax
import jax.numpy as jnp
from jax import lax
from jax.experimental import pallas as pl
from jax.experimental.pallas import tpu as pltpu
from jax.sharding import PartitionSpec as P

epsilon = 1e-06
smoothing = 0.05
exp2_factor = 1.0 / (smoothing * math.log(2.0))
log2_factor = smoothing * math.log(2.0)

f32 = jnp.float32
bf16 = jnp.bfloat16
i32 = jnp.int32

OWNERS = 32
SLOTS = 8
ENTRIES = OWNERS * SLOTS
QBLOCK = 4
LISTED = 16
QTOK = 32
TOKP = 256
PROJ = 128
P_DEV = 40
D_FEAT = 1152
META = 16
QROWS = QBLOCK * QTOK
QSTRIDE = QROWS + META
CHUNK = 8
LANES = CHUNK * QTOK
GRAD_ROWS = D_FEAT // OWNERS
GRAD_PAD = 48
RSTRIDE = QROWS
POSITIONS = 640
EMPTY_CHUNK = POSITIONS // CHUNK - 1
UNROLL = 4
MIB = 1 << 20
SMALL = pltpu.CompilerParams(vmem_limit_bytes=8 * MIB)


def iota(shape, dim):
    return lax.broadcasted_iota(i32, shape, dim)


def row_to_col(row, n):
    same = iota((n, n), 0) == iota((n, n), 1)
    return jnp.sum(jnp.where(same, jnp.broadcast_to(row, (n, n)), 0.0), axis=1, keepdims=True)


def col_to_row(col, n):
    same = iota((n, n), 0) == iota((n, n), 1)
    return jnp.sum(jnp.where(same, jnp.broadcast_to(col, (n, n)), 0.0), axis=0, keepdims=True)


def contract_first(a, b):
    return lax.dot_general(a, b, (((0,), (0,)), ((), ())), preferred_element_type=f32)


def contract_last(a, b):
    return lax.dot_general(a, b, (((1,), (1,)), ((), ())), preferred_element_type=f32)


def send_kernel(ids_ref, q_ref, out_ref):
    wide = q_ref[...].reshape(QROWS, PROJ).astype(f32)
    scale = lax.rsqrt(jnp.sum(wide * wide, axis=1, keepdims=True) + epsilon)
    emb = (wide * scale).astype(bf16)
    out_ref[:, 0:QROWS, :] = jnp.broadcast_to(emb[None], (OWNERS, QROWS, PROJ))
    ids = ids_ref[...].astype(f32)
    owner = jnp.floor((ids + 0.5) * (1.0 / P_DEV))
    local = ids - owner * P_DEV
    owner_col = jnp.concatenate([row_to_col(owner[q : q + 1], LISTED) for q in range(QBLOCK)], 0)
    local_col = jnp.concatenate([row_to_col(local[q : q + 1], LISTED) for q in range(QBLOCK)], 0)
    pairs = QBLOCK * LISTED
    lane = iota((pairs, 128), 1)
    entry = iota((pairs, 128), 0)
    hit = (owner_col.astype(i32) == lane).astype(f32)
    before = (iota((pairs, pairs), 1) < iota((pairs, pairs), 0)).astype(f32)
    rank = jnp.sum(
        hit * jnp.dot(before, hit, preferred_element_type=f32), axis=1, keepdims=True
    ).astype(i32)
    code = (entry // LISTED) * 2 + (entry % LISTED == 0).astype(i32)
    value = jnp.where(
        rank == lane,
        local_col + 1.0,
        jnp.where(rank + SLOTS == lane, code.astype(f32), 0.0),
    )
    value = jnp.where(lane < 2 * SLOTS, value, 0.0)
    meta = contract_first(hit, value)[0:OWNERS]
    out_ref[:, QROWS:QSTRIDE, :] = jnp.broadcast_to(
        meta[:, None, :], (OWNERS, META, PROJ)
    ).astype(bf16)


def send_queries(page_ids, queries):
    return pl.pallas_call(
        send_kernel,
        out_shape=jax.ShapeDtypeStruct((OWNERS, QSTRIDE, PROJ), bf16),
        compiler_params=SMALL,
        name="send_queries",
    )(page_ids, queries)


PROJ_ROWS = 1024
PROJ_SLOTS = 4
PROJ_STEPS = P_DEV * TOKP // PROJ_ROWS


def project_kernel(x_hbm, w_ref, proj_hbm, emb_hbm, x_ref, proj_ref, emb_ref, sems, proj_sems, emb_sems):
    def part(step):
        return pl.ds(step * PROJ_ROWS, PROJ_ROWS)

    def load(step):
        slot = step % PROJ_SLOTS
        return pltpu.make_async_copy(x_hbm.at[part(step)], x_ref.at[slot], sems.at[slot])

    def stores(step):
        return (
            pltpu.make_async_copy(proj_ref.at[part(step)], proj_hbm.at[part(step)], proj_sems.at[step]),
            pltpu.make_async_copy(emb_ref.at[part(step)], emb_hbm.at[part(step)], emb_sems.at[step]),
        )

    for step in range(PROJ_SLOTS):
        load(step).start()
    for step in range(PROJ_STEPS):
        load(step).wait()
        value = jnp.dot(x_ref[step % PROJ_SLOTS], w_ref[...], preferred_element_type=f32)
        if step + PROJ_SLOTS < PROJ_STEPS:
            load(step + PROJ_SLOTS).start()
        proj_ref[part(step), :] = value
        scale = lax.rsqrt(jnp.sum(value * value, axis=1, keepdims=True) + epsilon)
        emb_ref[part(step), :] = (value * scale).astype(bf16)
        for store in stores(step):
            store.start()
    for step in range(PROJ_STEPS):
        for store in stores(step):
            store.wait()


def project(rows, weight):
    total = rows.shape[0]
    vmem = pl.BlockSpec(memory_space=pltpu.VMEM)
    hbm = pl.BlockSpec(memory_space=pltpu.HBM)
    return pl.pallas_call(
        project_kernel,
        in_specs=[hbm, vmem],
        out_specs=[hbm, hbm],
        out_shape=[
            jax.ShapeDtypeStruct((total, PROJ), f32),
            jax.ShapeDtypeStruct((total, PROJ), bf16),
        ],
        scratch_shapes=[
            pltpu.VMEM((PROJ_SLOTS, PROJ_ROWS, D_FEAT), bf16),
            pltpu.VMEM((total, PROJ), f32),
            pltpu.VMEM((total, PROJ), bf16),
            pltpu.SemaphoreType.DMA((PROJ_SLOTS,)),
            pltpu.SemaphoreType.DMA((PROJ_STEPS,)),
            pltpu.SemaphoreType.DMA((PROJ_STEPS,)),
        ],
        compiler_params=pltpu.CompilerParams(vmem_limit_bytes=58 * MIB),
        cost_estimate=pl.CostEstimate(
            flops=2 * total * D_FEAT * PROJ,
            bytes_accessed=total * (2 * D_FEAT + 6 * PROJ),
            transcendentals=0,
        ),
        name="project",
    )(rows, weight)


def slot_columns(recv_ref):
    meta = recv_ref[...].reshape(OWNERS, QSTRIDE, PROJ)[:, QROWS:QSTRIDE, :].astype(f32)
    meta = meta[:, 0:SLOTS, :].reshape(ENTRIES, PROJ)
    lane = iota((ENTRIES, PROJ), 1)
    slot = iota((ENTRIES, PROJ), 0) % SLOTS
    page = jnp.sum(jnp.where(lane == slot, meta, 0.0), axis=1, keepdims=True).astype(i32) - 1
    code = jnp.sum(jnp.where(lane == slot + SLOTS, meta, 0.0), axis=1, keepdims=True).astype(i32)
    query = (iota((ENTRIES, 1), 0) // SLOTS) * QBLOCK + code // 2
    return page, query, code % 2


def plan_entries(page, query):
    valid = page >= 0
    page_f = page.astype(f32)
    page_row = col_to_row(page_f, ENTRIES)
    earlier = iota((ENTRIES, ENTRIES), 1) < iota((ENTRIES, ENTRIES), 0)
    rank = jnp.sum(
        jnp.where((page_f == page_row) & earlier, 1.0, 0.0), axis=1, keepdims=True
    )
    lane = iota((ENTRIES, 128), 1)
    on_page = (page == lane).astype(f32)
    count = jnp.sum(on_page, axis=0, keepdims=True)
    chunks = jnp.floor((count + (CHUNK - 1)) * (1.0 / CHUNK))
    upper = (iota((128, 128), 0) < iota((128, 128), 1)).astype(f32)
    start = jnp.dot(jnp.broadcast_to(chunks, (8, 128)), upper, preferred_element_type=f32)[0:1]
    position = jnp.sum(on_page * start, axis=1, keepdims=True) * CHUNK + rank
    position = jnp.where(valid, position, -1.0).astype(i32)
    at = position == iota((ENTRIES, POSITIONS), 1)
    entry_id = iota((ENTRIES, 1), 0)
    slot_row = jnp.sum(jnp.where(at, entry_id - ENTRIES, 0), axis=0, keepdims=True) + ENTRIES
    row_of = (query // QBLOCK) * QSTRIDE + (query % QBLOCK) * QTOK
    row_row = jnp.sum(jnp.where(at, row_of, 0), axis=0, keepdims=True)
    out_row = (query // QBLOCK) * RSTRIDE + (query % QBLOCK) * QTOK
    query_row = jnp.sum(jnp.where(at, out_row, 0), axis=0, keepdims=True)
    start_col = row_to_col(start, 128)[0:P_DEV]
    chunk_page = (
        jnp.sum(
            jnp.where(start_col <= iota((P_DEV, 128), 1).astype(f32), 1, 0), axis=0, keepdims=True
        )
        - 1
    ) * TOKP
    total = jnp.sum(chunks, axis=1, keepdims=True).astype(i32)
    pad = jnp.zeros((1, POSITIONS - 256), i32)
    last = jnp.concatenate(
        [chunk_page, jnp.broadcast_to(total, (1, 128)), pad], axis=1
    )
    return jnp.concatenate(
        [slot_row, row_row, query_row, last, jnp.zeros((4, POSITIONS), i32)], axis=0
    )


def load_queries(recv_ref, table_ref, chunk):
    parts = []
    for j in range(CHUNK):
        row = pl.multiple_of(table_ref[1, chunk * CHUNK + j], 16)
        parts.append(recv_ref[pl.ds(row, QTOK), :])
    return jnp.concatenate(parts, axis=0)


def page_rows(table_ref, chunk):
    return pl.ds(pl.multiple_of(table_ref[3, chunk], TOKP), TOKP)


def chunk_sims(recv_ref, emb_ref, table_ref, chunk):
    return contract_last(
        emb_ref[page_rows(table_ref, chunk), :], load_queries(recv_ref, table_ref, chunk)
    )


def chunk_before(chunk, back):
    return jnp.where(chunk < back, EMPTY_CHUNK, chunk - back)


def forward_kernel(
    recv_ref, emb_hbm, back_ref, table_out, exps_ref, emb_ref, table_ref, logs_of, sims_ref, sems
):
    emb_copy = pltpu.make_async_copy(emb_hbm, emb_ref, sems.at[1])
    emb_copy.start()
    page, query, positive = slot_columns(recv_ref)
    table_out[...] = plan_entries(page, query)
    copy = pltpu.make_async_copy(table_out, table_ref, sems.at[0])
    copy.start()
    sims_ref[...] = jnp.zeros(sims_ref.shape, f32)
    copy.wait()
    emb_copy.wait()
    group = iota((1, 128), 1) // QTOK

    def steps(step, carry):
        for u in range(UNROLL):
            chunk = UNROLL * step + u
            sims_ref[u % 2] = chunk_sims(recv_ref, emb_ref, table_ref, chunk)
            chunk = chunk_before(chunk, 1)
            expw = jnp.exp2(sims_ref[(u + 1) % 2] * exp2_factor)
            logs = jnp.log2(jnp.sum(expw, axis=0, keepdims=True))
            for j in range(CHUNK):
                tile = logs[:, (j // 4) * 128 : (j // 4) * 128 + 128]
                slot = table_ref[0, chunk * CHUNK + j]
                logs_of[pl.ds(slot, 1), :] = jnp.where(group == j % 4, tile, 0.0)
        return carry

    lax.fori_loop(0, (table_ref[3, 128] + 1 + UNROLL - 1) // UNROLL, steps, 0)
    valid = page >= 0
    scores = log2_factor * jnp.sum(logs_of[0:ENTRIES, :], axis=1, keepdims=True)
    scores = jnp.where(valid, scores, 0.0)
    exps = jnp.where(valid, jnp.exp(scores), 0.0)
    exps_ref[...] = jnp.broadcast_to(exps, (ENTRIES, 128))
    lane = iota((ENTRIES, 128), 1)
    sums = jnp.sum(jnp.where(query == lane, exps, 0.0), axis=0, keepdims=True)
    slot = iota((ENTRIES, 128), 0) % SLOTS
    spread = jnp.where(lane == slot, scores, 0.0).reshape(OWNERS, SLOTS, 128)
    spread = jnp.sum(spread, axis=1, keepdims=True)
    which = iota((OWNERS, SLOTS, 128), 1)
    back_ref[...] = jnp.where(
        which == 0, sums[None], jnp.where(which == 1, spread, 0.0)
    )


def forward(recv, emb):
    vmem = pl.BlockSpec(memory_space=pltpu.VMEM)
    return pl.pallas_call(
        forward_kernel,
        in_specs=[vmem, pl.BlockSpec(memory_space=pltpu.HBM)],
        out_specs=[vmem, vmem, vmem],
        out_shape=[
            jax.ShapeDtypeStruct((OWNERS, SLOTS, 128), f32),
            jax.ShapeDtypeStruct((8, POSITIONS), i32),
            jax.ShapeDtypeStruct((ENTRIES, 128), f32),
        ],
        scratch_shapes=[
            pltpu.VMEM((P_DEV * TOKP, PROJ), bf16),
            pltpu.SMEM((8, POSITIONS), i32),
            pltpu.VMEM((ENTRIES + 8, 128), f32),
            pltpu.VMEM((2, TOKP, LANES), f32),
            pltpu.SemaphoreType.DMA((2,)),
        ],
        compiler_params=pltpu.CompilerParams(vmem_limit_bytes=58 * MIB),
        name="forward",
    )(recv, emb)


FEAT_STEPS = 10
FEAT_SLOTS = 6
FEAT_ROWS = P_DEV * TOKP // FEAT_STEPS


def backward_kernel(
    table_ref, recv_ref, exps_ref, sums_ref, emb_hbm, proj_hbm, feat_hbm, out_ref,
    weight_of, page_acc, query_acc, emb_ref, proj_ref, grad_ref, feat_ref, sims_ref, grads_ref, sems,
):
    def feature_copy(step):
        part = pl.ds(step * FEAT_ROWS, FEAT_ROWS)
        slot = step % FEAT_SLOTS
        return pltpu.make_async_copy(feat_hbm.at[part], feat_ref.at[slot], sems.at[slot])

    emb_copy = pltpu.make_async_copy(emb_hbm, emb_ref, sems.at[FEAT_SLOTS])
    emb_copy.start()
    proj_copy = pltpu.make_async_copy(proj_hbm, proj_ref, sems.at[FEAT_SLOTS + 1])
    proj_copy.start()
    for step in range(FEAT_SLOTS):
        feature_copy(step).start()

    page, query, positive = slot_columns(recv_ref)
    sums = jnp.sum(sums_ref[...], axis=0)[0:1]
    lane = iota((ENTRIES, 128), 1)
    total = jnp.sum(jnp.where(query == lane, sums, 0.0), axis=1, keepdims=True)
    valid = page >= 0
    total = jnp.where(valid, total, 1.0)
    weight_of[0:ENTRIES, :] = jnp.where(
        valid, exps_ref[...] / total - positive.astype(f32), 0.0
    )
    weight_of[ENTRIES : ENTRIES + 8, :] = jnp.zeros((8, 128), f32)
    page_acc[...] = jnp.zeros(page_acc.shape, f32)
    query_acc[...] = jnp.zeros(query_acc.shape, f32)
    sims_ref[...] = jnp.zeros(sims_ref.shape, f32)
    grads_ref[...] = jnp.zeros(grads_ref.shape, bf16)
    emb_copy.wait()
    group = iota((1, 128), 1) // QTOK

    def chunk_weights(chunk):
        tiles = []
        for half in range(CHUNK // 4):
            tile = jnp.zeros((1, 128), f32)
            for j in range(4):
                slot = table_ref[0, chunk * CHUNK + half * 4 + j]
                tile = jnp.where(group == j, weight_of[pl.ds(slot, 1), :], tile)
            tiles.append(tile)
        return jnp.concatenate(tiles, axis=1)

    def steps(step, carry):
        for u in range(UNROLL):
            chunk = UNROLL * step + u
            now, last = u % 2, (u + 1) % 2
            sims_ref[now] = chunk_sims(recv_ref, emb_ref, table_ref, chunk)

            middle = chunk_before(chunk, 1)
            expw = jnp.exp2(sims_ref[last] * exp2_factor)
            ratio = chunk_weights(middle) / jnp.sum(expw, axis=0, keepdims=True)
            grads_ref[last] = (expw * ratio).astype(bf16)

            oldest = chunk_before(chunk, 2)
            rows = page_rows(table_ref, oldest)
            sim_grad = grads_ref[now]
            page_part = jnp.dot(
                sim_grad, load_queries(recv_ref, table_ref, oldest), preferred_element_type=f32
            )
            query_part = contract_first(sim_grad, emb_ref[rows, :])
            page_acc[rows, :] += page_part
            for j in range(CHUNK):
                at = pl.ds(pl.multiple_of(table_ref[2, oldest * CHUNK + j], QTOK), QTOK)
                query_acc[at, :] += query_part[j * QTOK : (j + 1) * QTOK]
        return carry

    lax.fori_loop(0, (table_ref[3, 128] + 2 + UNROLL - 1) // UNROLL, steps, 0)
    out_ref[:, 0:QROWS, :] = query_acc[...].astype(bf16).reshape(OWNERS, QROWS, PROJ)
    proj_copy.wait()

    def token_grads(step, carry):
        part = pl.ds(pl.multiple_of(step * 512, 512), 512)
        value = proj_ref[part, :]
        upstream = page_acc[part, :]
        scale = lax.rsqrt(jnp.sum(value * value, axis=1, keepdims=True) + epsilon)
        inner = jnp.sum(value * upstream, axis=1, keepdims=True)
        grad_ref[part, :] = (
            upstream * scale - value * (scale * scale * scale * inner)
        ).astype(bf16)
        return carry

    lax.fori_loop(0, P_DEV * TOKP // 512, token_grads, 0)
    grad = jnp.zeros((PROJ, D_FEAT), f32)
    for step in range(FEAT_STEPS):
        part = pl.ds(step * FEAT_ROWS, FEAT_ROWS)
        feature_copy(step).wait()
        grad += contract_first(grad_ref[part, :], feat_ref[step % FEAT_SLOTS])
        if step + FEAT_SLOTS < FEAT_STEPS:
            feature_copy(step + FEAT_SLOTS).start()
    grad = grad.T
    for owner in range(OWNERS):
        rows = grad[owner * GRAD_ROWS : (owner + 1) * GRAD_ROWS]
        rows = jnp.concatenate([rows, jnp.zeros((GRAD_PAD - GRAD_ROWS, PROJ), f32)], axis=0)
        out_ref[owner, QROWS : QROWS + GRAD_PAD, :] = rows.astype(bf16)


def backward(table, recv, exps, sums, emb, proj, rows):
    vmem = pl.BlockSpec(memory_space=pltpu.VMEM)
    hbm = pl.BlockSpec(memory_space=pltpu.HBM)
    return pl.pallas_call(
        backward_kernel,
        in_specs=[pl.BlockSpec(memory_space=pltpu.SMEM), vmem, vmem, vmem, hbm, hbm, hbm],
        out_specs=vmem,
        out_shape=jax.ShapeDtypeStruct((OWNERS, QROWS + GRAD_PAD, PROJ), bf16),
        scratch_shapes=[
            pltpu.VMEM((ENTRIES + 8, 128), f32),
            pltpu.VMEM((P_DEV * TOKP, PROJ), f32),
            pltpu.VMEM((OWNERS * QROWS, PROJ), f32),
            pltpu.VMEM((P_DEV * TOKP, PROJ), bf16),
            pltpu.VMEM((P_DEV * TOKP, PROJ), f32),
            pltpu.VMEM((P_DEV * TOKP, PROJ), bf16),
            pltpu.VMEM((FEAT_SLOTS, FEAT_ROWS, D_FEAT), bf16),
            pltpu.VMEM((2, TOKP, LANES), f32),
            pltpu.VMEM((2, TOKP, LANES), bf16),
            pltpu.SemaphoreType.DMA((FEAT_SLOTS + 2,)),
        ],
        compiler_params=pltpu.CompilerParams(vmem_limit_bytes=58 * MIB),
        name="backward",
    )(table, recv, exps, sums, emb, proj, rows)


def share_kernel(parts_ref, out_ref):
    out_ref[...] = jnp.sum(parts_ref[:, QROWS : QROWS + GRAD_PAD, :].astype(f32), axis=0)


def own_share(parts):
    return pl.pallas_call(
        share_kernel,
        out_shape=jax.ShapeDtypeStruct((GRAD_PAD, PROJ), f32),
        compiler_params=SMALL,
        name="own_share",
    )(parts)


def spread_kernel(a_ref, b_ref, c_ref, d_ref, out_ref):
    total = (a_ref[...] + b_ref[...]) + (c_ref[...] + d_ref[...])
    out_ref[...] = jnp.broadcast_to(total.astype(bf16)[None], out_ref.shape)


def spread_share(shares):
    return pl.pallas_call(
        spread_kernel,
        out_shape=jax.ShapeDtypeStruct((OWNERS, GRAD_PAD, PROJ), bf16),
        compiler_params=SMALL,
        name="spread_share",
    )(*shares)


def collect_kernel(parts_ref, out_ref):
    for owner in range(OWNERS):
        rows = parts_ref[owner].astype(f32)[0:GRAD_ROWS]
        out_ref[owner * GRAD_ROWS : (owner + 1) * GRAD_ROWS, :] = rows


def collect(parts):
    return pl.pallas_call(
        collect_kernel,
        out_shape=jax.ShapeDtypeStruct((D_FEAT, PROJ), f32),
        compiler_params=SMALL,
        name="collect",
    )(parts)


def query_kernel(parts_ref, q_ref, out_ref):
    upstream = jnp.sum(parts_ref[:, 0:QROWS, :].astype(f32), axis=0)
    wide = q_ref[...].reshape(QROWS, PROJ).astype(f32)
    scale = lax.rsqrt(jnp.sum(wide * wide, axis=1, keepdims=True) + epsilon)
    inner = jnp.sum(wide * upstream, axis=1, keepdims=True)
    out_ref[...] = (upstream * scale - wide * (scale * scale * scale * inner)).reshape(
        out_ref.shape
    )


def query_grads(parts, queries):
    return pl.pallas_call(
        query_kernel,
        out_shape=jax.ShapeDtypeStruct(queries.shape, f32),
        compiler_params=SMALL,
        name="query_grads",
    )(parts, queries)


def listed_scores(sums, page_ids):
    owner_of = page_ids.reshape(-1) // P_DEV
    hits = (owner_of[:, None] == jnp.arange(OWNERS, dtype=i32)[None, :]).astype(i32)
    rank_of = jnp.sum(jnp.cumsum(hits, axis=0) * hits, axis=1) - 1
    slots = sums[:, 1, 0:SLOTS]
    pick = (hits != 0)[:, :, None] & (rank_of[:, None] == jnp.arange(SLOTS, dtype=i32))[:, None, :]
    return jnp.sum(jnp.where(pick, slots[None], 0.0), axis=(1, 2)).reshape(page_ids.shape)


def exchange(values, axes):
    return lax.all_to_all(values, axes, split_axis=0, concat_axis=0, tiled=True)


def per_device(features, queries, proj_weight, page_ids):
    rows = features.reshape(P_DEV * TOKP, D_FEAT)
    recv = exchange(send_queries(page_ids, queries), "pages").reshape(OWNERS * QSTRIDE, PROJ)
    proj, emb = project(rows, proj_weight)
    back, table, exps = forward(recv, emb)
    sums = exchange(back, "pages")
    parts = exchange(backward(table, recv, exps, sums, emb, proj, rows), "pages")
    share = own_share(parts)
    replicas = lax.axis_size("rep")
    shares = [share] + [
        lax.ppermute(share, "rep", [(i, i ^ k) for i in range(replicas)]) for k in (1, 2, 3)
    ]
    grad_proj = collect(exchange(spread_share(shares), "pages"))
    grad_query = query_grads(parts, queries)
    scores = listed_scores(sums, page_ids)
    return (scores, grad_query, grad_proj)


def solution(mesh):
    in_specs = (
        P("pages", None, None),
        P(("pages", "rep"), None, None),
        P(),
        P(("pages", "rep"), None),
    )
    out_specs = (P(("pages", "rep"), None), P(("pages", "rep"), None, None), P())
    return jax.shard_map(
        per_device, mesh=mesh, in_specs=in_specs, out_specs=out_specs, check_vma=False
    )
```

```python
import math

import jax
import jax.numpy as jnp
from jax import lax
from jax.experimental import pallas as pl
from jax.experimental.pallas import tpu as pltpu
from jax.sharding import PartitionSpec as P

epsilon = 1e-06
smoothing = 0.05
exp2_factor = 1.0 / (smoothing * math.log(2.0))
log2_factor = smoothing * math.log(2.0)

f32 = jnp.float32
bf16 = jnp.bfloat16
i32 = jnp.int32

OWNERS = 32
SLOTS = 8
ENTRIES = OWNERS * SLOTS
QBLOCK = 4
LISTED = 16
QTOK = 32
TOKP = 256
PROJ = 128
P_DEV = 40
D_FEAT = 1152
META = 16
QROWS = QBLOCK * QTOK
QSTRIDE = QROWS + META
CHUNK = 8
LANES = CHUNK * QTOK
GRAD_ROWS = D_FEAT // OWNERS
GRAD_PAD = 48
CHIPS = OWNERS // 2
POSITIONS = 640
EMPTY_CHUNK = POSITIONS // CHUNK - 1
UNROLL = 6
MIB = 1 << 20
SMALL = pltpu.CompilerParams(vmem_limit_bytes=8 * MIB)


def iota(shape, dim):
    return lax.broadcasted_iota(i32, shape, dim)


def row_to_col(row, n):
    same = iota((n, n), 0) == iota((n, n), 1)
    return jnp.sum(jnp.where(same, jnp.broadcast_to(row, (n, n)), 0.0), axis=1, keepdims=True)


def col_to_row(col, n):
    same = iota((n, n), 0) == iota((n, n), 1)
    return jnp.sum(jnp.where(same, jnp.broadcast_to(col, (n, n)), 0.0), axis=0, keepdims=True)


def contract_first(a, b):
    return lax.dot_general(a, b, (((0,), (0,)), ((), ())), preferred_element_type=f32)


def contract_last(a, b):
    return lax.dot_general(a, b, (((1,), (1,)), ((), ())), preferred_element_type=f32)


def send_kernel(ids_ref, q_ref, out_ref):
    wide = q_ref[...].reshape(QROWS, PROJ).astype(f32)
    scale = lax.rsqrt(jnp.sum(wide * wide, axis=1, keepdims=True) + epsilon)
    emb = (wide * scale).astype(bf16)
    out_ref[:, 0:QROWS, :] = jnp.broadcast_to(emb[None], (CHIPS, QROWS, PROJ))
    ids = ids_ref[...].astype(f32)
    owner = jnp.floor((ids + 0.5) * (1.0 / P_DEV))
    local = ids - owner * P_DEV
    owner_col = jnp.concatenate([row_to_col(owner[q : q + 1], LISTED) for q in range(QBLOCK)], 0)
    local_col = jnp.concatenate([row_to_col(local[q : q + 1], LISTED) for q in range(QBLOCK)], 0)
    pairs = QBLOCK * LISTED
    lane = iota((pairs, 128), 1)
    entry = iota((pairs, 128), 0)
    hit = (owner_col.astype(i32) == lane).astype(f32)
    before = (iota((pairs, pairs), 1) < iota((pairs, pairs), 0)).astype(f32)
    rank = jnp.sum(
        hit * jnp.dot(before, hit, preferred_element_type=f32), axis=1, keepdims=True
    ).astype(i32)
    code = (entry // LISTED) * 2 + (entry % LISTED == 0).astype(i32)
    base = rank + 2 * SLOTS * (owner_col.astype(i32) % 2)
    value = jnp.where(
        base == lane,
        local_col + 1.0,
        jnp.where(base + SLOTS == lane, code.astype(f32), 0.0),
    )
    on_chip = (owner_col.astype(i32) // 2 == lane).astype(f32)
    meta = contract_first(on_chip, value)[0:CHIPS]
    out_ref[:, QROWS:QSTRIDE, :] = jnp.broadcast_to(
        meta[:, None, :], (CHIPS, META, PROJ)
    ).astype(bf16)


def send_queries(page_ids, queries):
    return pl.pallas_call(
        send_kernel,
        out_shape=jax.ShapeDtypeStruct((CHIPS, QSTRIDE, PROJ), bf16),
        compiler_params=pltpu.CompilerParams(vmem_limit_bytes=58 * MIB),
        name="send_queries",
    )(page_ids, queries)


PROJ_ROWS = 2048
PROJ_SUB = 512
PROJ_STEPS = P_DEV * TOKP // PROJ_ROWS


def project_kernel(
    x_hbm, w_ref, emb_hbm, rest_hbm, scale_out, x_ref, value_ref, emb_ref, rest_ref, sems, emb_sems, rest_sems
):
    def part(step):
        return pl.ds(step * PROJ_ROWS, PROJ_ROWS)

    def load(step):
        return pltpu.make_async_copy(x_hbm.at[part(step)], x_ref.at[part(step)], sems.at[step])

    def stores(step):
        return (
            pltpu.make_async_copy(emb_ref.at[part(step)], emb_hbm.at[part(step)], emb_sems.at[step]),
            pltpu.make_async_copy(rest_ref.at[part(step)], rest_hbm.at[part(step)], rest_sems.at[step]),
        )

    def normalize(at):
        rows = pl.ds(at, PROJ_SUB)
        value = value_ref[rows, :]
        scale = lax.rsqrt(jnp.sum(value * value, axis=1, keepdims=True) + epsilon)
        unit = value * scale
        emb = unit.astype(bf16)
        emb_ref[rows, :] = emb
        rest_ref[rows, :] = (unit - emb.astype(f32)).astype(bf16)
        for block in range(PROJ_SUB // 128):
            row = at // 128 + block
            scale_out[row : row + 1, :] = col_to_row(scale[block * 128 : block * 128 + 128], 128)

    for step in range(PROJ_STEPS):
        load(step).start()
    for step in range(PROJ_STEPS):
        load(step).wait()
        first = step * PROJ_ROWS
        for at in range(first, first + PROJ_ROWS, PROJ_SUB):
            value_ref[pl.ds(at, PROJ_SUB), :] = jnp.dot(
                x_ref[pl.ds(at, PROJ_SUB), :], w_ref[...], preferred_element_type=f32
            )
            if at > first:
                normalize(at - PROJ_SUB)
        normalize(first + PROJ_ROWS - PROJ_SUB)
        for store in stores(step):
            store.start()
    for step in range(PROJ_STEPS):
        for store in stores(step):
            store.wait()


def project(rows, weight):
    total = rows.shape[0]
    vmem = pl.BlockSpec(memory_space=pltpu.VMEM)
    hbm = pl.BlockSpec(memory_space=pltpu.HBM)
    return pl.pallas_call(
        project_kernel,
        in_specs=[hbm, vmem],
        out_specs=[hbm, hbm, vmem],
        out_shape=[
            jax.ShapeDtypeStruct((total, PROJ), bf16),
            jax.ShapeDtypeStruct((total, PROJ), bf16),
            jax.ShapeDtypeStruct((total // 128, 128), f32),
        ],
        scratch_shapes=[
            pltpu.VMEM((total, D_FEAT), bf16),
            pltpu.VMEM((total, PROJ), f32),
            pltpu.VMEM((total, PROJ), bf16),
            pltpu.VMEM((total, PROJ), bf16),
            pltpu.SemaphoreType.DMA((PROJ_STEPS,)),
            pltpu.SemaphoreType.DMA((PROJ_STEPS,)),
            pltpu.SemaphoreType.DMA((PROJ_STEPS,)),
        ],
        compiler_params=pltpu.CompilerParams(vmem_limit_bytes=58 * MIB),
        cost_estimate=pl.CostEstimate(
            flops=2 * total * D_FEAT * PROJ,
            bytes_accessed=total * (2 * D_FEAT + 4 * PROJ),
            transcendentals=0,
        ),
        name="project",
    )(rows, weight)


def receive(parts, recv_ref, sems):
    half = CHIPS * QSTRIDE
    copies = [
        pltpu.make_async_copy(part, recv_ref.at[pl.ds(i * half, half)], sems.at[i])
        for i, part in enumerate(parts)
    ]
    for copy in copies:
        copy.start()
    return copies


def slot_columns(recv_ref, core):
    meta = recv_ref[...].reshape(OWNERS, QSTRIDE, PROJ)[:, QROWS:QSTRIDE, :].astype(f32)
    meta = meta[:, 0:SLOTS, :].reshape(ENTRIES, PROJ)
    lane = iota((ENTRIES, PROJ), 1) - 2 * SLOTS * core
    slot = iota((ENTRIES, PROJ), 0) % SLOTS
    page = jnp.sum(jnp.where(lane == slot, meta, 0.0), axis=1, keepdims=True).astype(i32) - 1
    code = jnp.sum(jnp.where(lane == slot + SLOTS, meta, 0.0), axis=1, keepdims=True).astype(i32)
    source = iota((ENTRIES, 1), 0) // SLOTS
    other = source // CHIPS
    owner = 2 * (source % CHIPS) + jnp.where(other == 0, core, 1 - core)
    return page, owner * QBLOCK + code // 2, code // 2, code % 2


def plan_entries(page, of_source):
    valid = page >= 0
    page_f = page.astype(f32)
    page_row = col_to_row(page_f, ENTRIES)
    earlier = iota((ENTRIES, ENTRIES), 1) < iota((ENTRIES, ENTRIES), 0)
    rank = jnp.sum(
        jnp.where((page_f == page_row) & earlier, 1.0, 0.0), axis=1, keepdims=True
    )
    lane = iota((ENTRIES, 128), 1)
    on_page = (page == lane).astype(f32)
    count = jnp.sum(on_page, axis=0, keepdims=True)
    chunks = jnp.floor((count + (CHUNK - 1)) * (1.0 / CHUNK))
    upper = (iota((128, 128), 0) < iota((128, 128), 1)).astype(f32)
    start = jnp.dot(jnp.broadcast_to(chunks, (8, 128)), upper, preferred_element_type=f32)[0:1]
    position = jnp.sum(on_page * start, axis=1, keepdims=True) * CHUNK + rank
    position = jnp.where(valid, position, -1.0).astype(i32)
    at = position == iota((ENTRIES, POSITIONS), 1)
    entry_id = iota((ENTRIES, 1), 0)
    slot_row = jnp.sum(jnp.where(at, entry_id - ENTRIES, 0), axis=0, keepdims=True) + ENTRIES
    source = entry_id // SLOTS
    row_of = source * QSTRIDE + of_source * QTOK
    row_row = jnp.sum(jnp.where(at, row_of, 0), axis=0, keepdims=True)
    out_row = source * QROWS + of_source * QTOK
    query_row = jnp.sum(jnp.where(at, out_row, 0), axis=0, keepdims=True)
    start_col = row_to_col(start, 128)[0:P_DEV]
    chunk_page = (
        jnp.sum(
            jnp.where(start_col <= iota((P_DEV, 128), 1).astype(f32), 1, 0), axis=0, keepdims=True
        )
        - 1
    ) * TOKP
    total = jnp.sum(chunks, axis=1, keepdims=True).astype(i32)
    pad = jnp.zeros((1, POSITIONS - 256), i32)
    last = jnp.concatenate(
        [chunk_page, jnp.broadcast_to(total, (1, 128)), pad], axis=1
    )
    return jnp.concatenate(
        [slot_row, row_row, query_row, last, jnp.zeros((4, POSITIONS), i32)], axis=0
    )


def load_queries(recv_ref, table_ref, chunk):
    parts = []
    for j in range(CHUNK):
        row = pl.multiple_of(table_ref[1, chunk * CHUNK + j], 16)
        parts.append(recv_ref[pl.ds(row, QTOK), :])
    return jnp.concatenate(parts, axis=0)


def page_rows(table_ref, chunk):
    return pl.ds(pl.multiple_of(table_ref[3, chunk], TOKP), TOKP)


def chunk_sims(recv_ref, emb_ref, table_ref, chunk):
    return contract_last(
        emb_ref[page_rows(table_ref, chunk), :], load_queries(recv_ref, table_ref, chunk)
    )


def chunk_before(chunk, back):
    return jnp.where(chunk < back, EMPTY_CHUNK, chunk - back)


def forward_kernel(
    core_ref, own_any, other_any, emb_hbm, back_ref, table_out, exps_ref,
    recv_ref, emb_ref, table_ref, logs_of, sims_ref, sems, recv_sems,
):
    emb_copy = pltpu.make_async_copy(emb_hbm, emb_ref, sems.at[1])
    core = core_ref[0]
    received = receive((own_any, other_any), recv_ref, recv_sems)
    emb_copy.start()
    sims_ref[...] = jnp.zeros(sims_ref.shape, f32)
    for copy in received:
        copy.wait()
    page, query, of_source, positive = slot_columns(recv_ref, core)
    table_out[...] = plan_entries(page, of_source)
    copy = pltpu.make_async_copy(table_out, table_ref, sems.at[0])
    copy.start()
    copy.wait()
    emb_copy.wait()
    group = iota((1, 128), 1) // QTOK

    def steps(step, carry):
        for u in range(UNROLL):
            chunk = UNROLL * step + u
            sims_ref[u % 2] = chunk_sims(recv_ref, emb_ref, table_ref, chunk)
            chunk = chunk_before(chunk, 1)
            expw = jnp.exp2(sims_ref[(u + 1) % 2] * exp2_factor)
            logs = jnp.log2(jnp.sum(expw, axis=0, keepdims=True))
            for j in range(CHUNK):
                tile = logs[:, (j // 4) * 128 : (j // 4) * 128 + 128]
                slot = table_ref[0, chunk * CHUNK + j]
                logs_of[pl.ds(slot, 1), :] = jnp.where(group == j % 4, tile, 0.0)
        return carry

    lax.fori_loop(0, (table_ref[3, 128] + 1 + UNROLL - 1) // UNROLL, steps, 0)
    valid = page >= 0
    scores = log2_factor * jnp.sum(logs_of[0:ENTRIES, :], axis=1, keepdims=True)
    scores = jnp.where(valid, scores, 0.0)
    exps = jnp.where(valid, jnp.exp(scores), 0.0)
    exps_ref[...] = jnp.broadcast_to(exps, (ENTRIES, 128))
    lane = iota((ENTRIES, 128), 1)
    sums = jnp.sum(jnp.where(query == lane, exps, 0.0), axis=0, keepdims=True)
    slot = iota((ENTRIES, 128), 0) % SLOTS
    spread = jnp.where(lane == slot, scores, 0.0).reshape(OWNERS, SLOTS, 128)
    spread = jnp.sum(spread, axis=1, keepdims=True)
    which = iota((OWNERS, SLOTS, 128), 1)
    result = jnp.where(which == 0, sums[None], jnp.where(which == 1, spread, 0.0))
    own, other = result[0:CHIPS], result[CHIPS:OWNERS]
    back_ref[:, 0] = jnp.where(core == 0, own, other)
    back_ref[:, 1] = jnp.where(core == 0, other, own)


def forward(core, own, other, emb):
    vmem = pl.BlockSpec(memory_space=pltpu.VMEM)
    place = pl.BlockSpec(memory_space=pl.ANY)
    return pl.pallas_call(
        forward_kernel,
        in_specs=[
            pl.BlockSpec(memory_space=pltpu.SMEM),
            place,
            place,
            pl.BlockSpec(memory_space=pltpu.HBM),
        ],
        out_specs=[vmem, vmem, vmem],
        out_shape=[
            jax.ShapeDtypeStruct((CHIPS, 2, SLOTS, 128), f32),
            jax.ShapeDtypeStruct((8, POSITIONS), i32),
            jax.ShapeDtypeStruct((ENTRIES, 128), f32),
        ],
        scratch_shapes=[
            pltpu.VMEM((OWNERS * QSTRIDE, PROJ), bf16),
            pltpu.VMEM((P_DEV * TOKP, PROJ), bf16),
            pltpu.SMEM((8, POSITIONS), i32),
            pltpu.VMEM((ENTRIES + 8, 128), f32),
            pltpu.VMEM((2, TOKP, LANES), f32),
            pltpu.SemaphoreType.DMA((2,)),
            pltpu.SemaphoreType.DMA((2,)),
        ],
        compiler_params=pltpu.CompilerParams(vmem_limit_bytes=58 * MIB),
        name="forward",
    )(core, own, other, emb)


FEAT_STEPS = 5
FEAT_SUB = 1024
FEAT_ROWS = P_DEV * TOKP // FEAT_STEPS


def backward_kernel(
    core_ref, table_ref, exps_ref, sums_ref, scale_ref, own_any, other_any, emb_hbm, rest_hbm, feat_hbm,
    keep_ref, give_ref, recv_ref, weight_of, page_acc, query_acc, emb_ref, rest_ref, grad_ref, feat_ref, sims_ref, grads_ref, sems, recv_sems,
):
    def feature_copy(step):
        part = pl.ds(step * FEAT_ROWS, FEAT_ROWS)
        return pltpu.make_async_copy(feat_hbm.at[part], feat_ref.at[part], sems.at[step])

    emb_copy = pltpu.make_async_copy(emb_hbm, emb_ref, sems.at[FEAT_STEPS])
    received = receive((own_any, other_any), recv_ref, recv_sems)
    emb_copy.start()
    rest_copy = pltpu.make_async_copy(rest_hbm, rest_ref, sems.at[FEAT_STEPS + 1])

    page_acc[...] = jnp.zeros(page_acc.shape, f32)
    query_acc[...] = jnp.zeros(query_acc.shape, f32)
    sims_ref[...] = jnp.zeros(sims_ref.shape, f32)
    grads_ref[...] = jnp.zeros(grads_ref.shape, bf16)
    for copy in received:
        copy.wait()
    page, query, of_source, positive = slot_columns(recv_ref, core_ref[0])
    sums = jnp.sum(sums_ref[...], axis=0)[0:1]
    lane = iota((ENTRIES, 128), 1)
    total = jnp.sum(jnp.where(query == lane, sums, 0.0), axis=1, keepdims=True)
    valid = page >= 0
    total = jnp.where(valid, total, 1.0)
    weight_of[0:ENTRIES, :] = jnp.where(
        valid, exps_ref[...] / total - positive.astype(f32), 0.0
    )
    weight_of[ENTRIES : ENTRIES + 8, :] = jnp.zeros((8, 128), f32)
    emb_copy.wait()
    rest_copy.start()
    for step in range(FEAT_STEPS):
        feature_copy(step).start()
    group = iota((1, 128), 1) // QTOK

    def chunk_weights(chunk):
        tiles = []
        for half in range(CHUNK // 4):
            tile = jnp.zeros((1, 128), f32)
            for j in range(4):
                slot = table_ref[0, chunk * CHUNK + half * 4 + j]
                tile = jnp.where(group == j, weight_of[pl.ds(slot, 1), :], tile)
            tiles.append(tile)
        return jnp.concatenate(tiles, axis=1)

    def steps(step, carry):
        for u in range(UNROLL):
            chunk = UNROLL * step + u
            now, last = u % 2, (u + 1) % 2
            sims_ref[now] = chunk_sims(recv_ref, emb_ref, table_ref, chunk)

            middle = chunk_before(chunk, 1)
            expw = jnp.exp2(sims_ref[last] * exp2_factor)
            ratio = chunk_weights(middle) / jnp.sum(expw, axis=0, keepdims=True)
            grads_ref[last] = (expw * ratio).astype(bf16)

            oldest = chunk_before(chunk, 2)
            rows = page_rows(table_ref, oldest)
            sim_grad = grads_ref[now]
            page_part = jnp.dot(
                sim_grad, load_queries(recv_ref, table_ref, oldest), preferred_element_type=f32
            )
            query_part = contract_first(sim_grad, emb_ref[rows, :])
            page_acc[rows, :] += page_part
            for j in range(CHUNK):
                at = pl.ds(pl.multiple_of(table_ref[2, oldest * CHUNK + j], QTOK), QTOK)
                query_acc[at, :] += query_part[j * QTOK : (j + 1) * QTOK]
        return carry

    lax.fori_loop(0, (table_ref[3, 128] + 2 + UNROLL - 1) // UNROLL, steps, 0)
    half = CHIPS * QROWS
    for ref, at in ((keep_ref, 0), (give_ref, half)):
        ref[:, 0:QROWS, :] = query_acc[at : at + half, :].astype(bf16).reshape(CHIPS, QROWS, PROJ)
    rest_copy.wait()

    def token_grads(at):
        for block in range(at // 128, (at + FEAT_SUB) // 128):
            part = pl.ds(block * 128, 128)
            unit = emb_ref[part, :].astype(f32) + rest_ref[part, :].astype(f32)
            upstream = page_acc[part, :]
            scale = row_to_col(scale_ref[block : block + 1, :], 128)
            inner = jnp.sum(unit * upstream, axis=1, keepdims=True)
            grad_ref[part, :] = (scale * (upstream - unit * inner)).astype(bf16)

    total = P_DEV * TOKP
    grad = jnp.zeros((PROJ, D_FEAT), f32)
    token_grads(0)
    for at in range(0, total, FEAT_SUB):
        if at % FEAT_ROWS == 0:
            feature_copy(at // FEAT_ROWS).wait()
        if at + FEAT_SUB < total:
            token_grads(at + FEAT_SUB)
        part = pl.ds(at, FEAT_SUB)
        grad += contract_first(grad_ref[part, :], feat_ref[part, :])
    grad = grad.T
    pad = jnp.zeros((GRAD_PAD - GRAD_ROWS, PROJ), f32)
    first_core = core_ref[0] == 0
    for chip in range(CHIPS):
        at = 2 * chip * GRAD_ROWS
        even = jnp.concatenate([grad[at : at + GRAD_ROWS], pad], axis=0)
        odd = jnp.concatenate([grad[at + GRAD_ROWS : at + 2 * GRAD_ROWS], pad], axis=0)
        rows = pl.ds(QROWS, GRAD_PAD)
        keep_ref[chip, rows, :] = jnp.where(first_core, even, odd).astype(bf16)
        give_ref[chip, rows, :] = jnp.where(first_core, odd, even).astype(bf16)


def backward(core, table, exps, sums, scale, own, other, emb, rest, rows):
    vmem = pl.BlockSpec(memory_space=pltpu.VMEM)
    hbm = pl.BlockSpec(memory_space=pltpu.HBM)
    smem = pl.BlockSpec(memory_space=pltpu.SMEM)
    place = pl.BlockSpec(memory_space=pl.ANY)
    return pl.pallas_call(
        backward_kernel,
        in_specs=[smem, smem, vmem, vmem, vmem, place, place, hbm, hbm, hbm],
        out_specs=[vmem, vmem],
        out_shape=[jax.ShapeDtypeStruct((CHIPS, QROWS + GRAD_PAD, PROJ), bf16)] * 2,
        scratch_shapes=[
            pltpu.VMEM((OWNERS * QSTRIDE, PROJ), bf16),
            pltpu.VMEM((ENTRIES + 8, 128), f32),
            pltpu.VMEM((P_DEV * TOKP, PROJ), f32),
            pltpu.VMEM((OWNERS * QROWS, PROJ), f32),
            pltpu.VMEM((P_DEV * TOKP, PROJ), bf16),
            pltpu.VMEM((P_DEV * TOKP, PROJ), bf16),
            pltpu.VMEM((P_DEV * TOKP, PROJ), bf16),
            pltpu.VMEM((P_DEV * TOKP, D_FEAT), bf16),
            pltpu.VMEM((2, TOKP, LANES), f32),
            pltpu.VMEM((2, TOKP, LANES), bf16),
            pltpu.SemaphoreType.DMA((FEAT_STEPS + 2,)),
            pltpu.SemaphoreType.DMA((2,)),
        ],
        compiler_params=pltpu.CompilerParams(vmem_limit_bytes=58 * MIB),
        name="backward",
    )(core, table, exps, sums, scale, own, other, emb, rest, rows)


def pair_kernel(a_ref, b_ref, out_ref):
    out_ref[...] = (a_ref[...].astype(f32) + b_ref[...].astype(f32)).astype(bf16)


def pair_sum(a, b):
    return pl.pallas_call(
        pair_kernel,
        out_shape=jax.ShapeDtypeStruct(a.shape, bf16),
        compiler_params=SMALL,
        name="pair_sum",
    )(a, b)


def share_kernel(parts_ref, out_ref):
    out_ref[...] = jnp.sum(parts_ref[:, QROWS : QROWS + GRAD_PAD, :].astype(f32), axis=0)


def own_share(parts):
    return pl.pallas_call(
        share_kernel,
        out_shape=jax.ShapeDtypeStruct((GRAD_PAD, PROJ), f32),
        compiler_params=SMALL,
        name="own_share",
    )(parts)


def spread_kernel(a_ref, b_ref, c_ref, d_ref, out_ref):
    total = (a_ref[...] + b_ref[...]) + (c_ref[...] + d_ref[...])
    out_ref[...] = jnp.broadcast_to(total.astype(bf16)[None], out_ref.shape)


def spread_share(shares):
    return pl.pallas_call(
        spread_kernel,
        out_shape=jax.ShapeDtypeStruct((OWNERS, GRAD_PAD, PROJ), bf16),
        compiler_params=SMALL,
        name="spread_share",
    )(*shares)


def collect_kernel(parts_ref, out_ref):
    for owner in range(OWNERS):
        rows = parts_ref[owner].astype(f32)[0:GRAD_ROWS]
        out_ref[owner * GRAD_ROWS : (owner + 1) * GRAD_ROWS, :] = rows


def collect(parts):
    return pl.pallas_call(
        collect_kernel,
        out_shape=jax.ShapeDtypeStruct((D_FEAT, PROJ), f32),
        compiler_params=SMALL,
        name="collect",
    )(parts)


def query_kernel(parts_ref, q_ref, out_ref):
    upstream = jnp.sum(parts_ref[:, 0:QROWS, :].astype(f32), axis=0)
    wide = q_ref[...].reshape(QROWS, PROJ).astype(f32)
    scale = lax.rsqrt(jnp.sum(wide * wide, axis=1, keepdims=True) + epsilon)
    inner = jnp.sum(wide * upstream, axis=1, keepdims=True)
    out_ref[...] = (upstream * scale - wide * (scale * scale * scale * inner)).reshape(
        out_ref.shape
    )


def query_grads(parts, queries):
    return pl.pallas_call(
        query_kernel,
        out_shape=jax.ShapeDtypeStruct(queries.shape, f32),
        compiler_params=SMALL,
        name="query_grads",
    )(parts, queries)


def listed_scores(sums, page_ids):
    owner_of = page_ids.reshape(-1) // P_DEV
    hits = (owner_of[:, None] == jnp.arange(OWNERS, dtype=i32)[None, :]).astype(i32)
    rank_of = jnp.sum(jnp.cumsum(hits, axis=0) * hits, axis=1) - 1
    slots = sums[:, 1, 0:SLOTS]
    pick = (hits != 0)[:, :, None] & (rank_of[:, None] == jnp.arange(SLOTS, dtype=i32))[:, None, :]
    return jnp.sum(jnp.where(pick, slots[None], 0.0), axis=(1, 2)).reshape(page_ids.shape)


def exchange(values, axes, groups=None):
    return lax.all_to_all(
        values, axes, split_axis=0, concat_axis=0, axis_index_groups=groups, tiled=True
    )


def per_device(features, queries, proj_weight, page_ids):
    rows = features.reshape(P_DEV * TOKP, D_FEAT)
    same_core = [list(range(first, OWNERS, 2)) for first in range(2)]
    other_core = [(i, i ^ 1) for i in range(OWNERS)]
    core = (lax.axis_index("pages") % 2).astype(i32).reshape(1)
    own = exchange(send_queries(page_ids, queries), "pages", same_core)
    own, emb, rest, scale = lax.optimization_barrier((own, *project(rows, proj_weight)))
    other = lax.ppermute(own, "pages", other_core)
    own = own.reshape(CHIPS * QSTRIDE, PROJ)
    other = other.reshape(CHIPS * QSTRIDE, PROJ)
    back, table, exps = forward(core, own, other, emb)
    sums = exchange(back.reshape(OWNERS, SLOTS, 128), "pages")
    keep, give = backward(core, table, exps, sums, scale, own, other, emb, rest, rows)
    taken = lax.ppermute(give, "pages", other_core)
    parts = exchange(pair_sum(keep, taken), "pages", same_core)
    share = own_share(parts)
    replicas = lax.axis_size("rep")
    shares = [share] + [
        lax.ppermute(share, "rep", [(i, i ^ k) for i in range(replicas)]) for k in (1, 2, 3)
    ]
    grad_proj = collect(exchange(spread_share(shares), "pages"))
    grad_query = query_grads(parts, queries)
    scores = listed_scores(sums, page_ids)
    return (scores, grad_query, grad_proj)


def solution(mesh):
    in_specs = (
        P("pages", None, None),
        P(("pages", "rep"), None, None),
        P(),
        P(("pages", "rep"), None),
    )
    out_specs = (P(("pages", "rep"), None), P(("pages", "rep"), None, None), P())
    return jax.shard_map(
        per_device, mesh=mesh, in_specs=in_specs, out_specs=out_specs, check_vma=False
    )
```

```python
import math

import jax
import jax.numpy as jnp
from jax import lax
from jax.experimental import pallas as pl
from jax.experimental.pallas import tpu as pltpu
from jax.sharding import PartitionSpec as P

epsilon = 1e-06
smoothing = 0.05
exp2_factor = 1.0 / (smoothing * math.log(2.0))
log2_factor = smoothing * math.log(2.0)

f32 = jnp.float32
bf16 = jnp.bfloat16
i32 = jnp.int32

OWNERS = 32
SLOTS = 8
ENTRIES = OWNERS * SLOTS
QBLOCK = 4
LISTED = 16
QTOK = 32
TOKP = 256
PROJ = 128
P_DEV = 40
D_FEAT = 1152
META = 16
QROWS = QBLOCK * QTOK
QSTRIDE = QROWS + META
CHUNK = 8
LANES = CHUNK * QTOK
GRAD_ROWS = D_FEAT // OWNERS
GRAD_PAD = 48
CHIPS = OWNERS // 2
POSITIONS = 640
EMPTY_CHUNK = POSITIONS // CHUNK - 1
UNROLL = 6
MIB = 1 << 20
SMALL = pltpu.CompilerParams(vmem_limit_bytes=8 * MIB)


def iota(shape, dim):
    return lax.broadcasted_iota(i32, shape, dim)


def row_to_col(row, n):
    same = iota((n, n), 0) == iota((n, n), 1)
    return jnp.sum(jnp.where(same, jnp.broadcast_to(row, (n, n)), 0.0), axis=1, keepdims=True)


def col_to_row(col, n):
    same = iota((n, n), 0) == iota((n, n), 1)
    return jnp.sum(jnp.where(same, jnp.broadcast_to(col, (n, n)), 0.0), axis=0, keepdims=True)


def contract_first(a, b):
    return lax.dot_general(a, b, (((0,), (0,)), ((), ())), preferred_element_type=f32)


def contract_last(a, b):
    return lax.dot_general(a, b, (((1,), (1,)), ((), ())), preferred_element_type=f32)


def send_kernel(ids_ref, q_ref, out_ref):
    wide = q_ref[...].reshape(QROWS, PROJ).astype(f32)
    scale = lax.rsqrt(jnp.sum(wide * wide, axis=1, keepdims=True) + epsilon)
    emb = (wide * scale).astype(bf16)
    out_ref[:, 0:QROWS, :] = jnp.broadcast_to(emb[None], (CHIPS, QROWS, PROJ))
    ids = ids_ref[...].astype(f32)
    owner = jnp.floor((ids + 0.5) * (1.0 / P_DEV))
    local = ids - owner * P_DEV
    owner_col = jnp.concatenate([row_to_col(owner[q : q + 1], LISTED) for q in range(QBLOCK)], 0)
    local_col = jnp.concatenate([row_to_col(local[q : q + 1], LISTED) for q in range(QBLOCK)], 0)
    pairs = QBLOCK * LISTED
    lane = iota((pairs, 128), 1)
    entry = iota((pairs, 128), 0)
    hit = (owner_col.astype(i32) == lane).astype(f32)
    before = (iota((pairs, pairs), 1) < iota((pairs, pairs), 0)).astype(f32)
    rank = jnp.sum(
        hit * jnp.dot(before, hit, preferred_element_type=f32), axis=1, keepdims=True
    ).astype(i32)
    code = (entry // LISTED) * 2 + (entry % LISTED == 0).astype(i32)
    base = rank + 2 * SLOTS * (owner_col.astype(i32) % 2)
    value = jnp.where(
        base == lane,
        local_col + 1.0,
        jnp.where(base + SLOTS == lane, code.astype(f32), 0.0),
    )
    on_chip = (owner_col.astype(i32) // 2 == lane).astype(f32)
    meta = contract_first(on_chip, value)[0:CHIPS]
    out_ref[:, QROWS:QSTRIDE, :] = jnp.broadcast_to(
        meta[:, None, :], (CHIPS, META, PROJ)
    ).astype(bf16)


def send_queries(page_ids, queries):
    return pl.pallas_call(
        send_kernel,
        out_shape=jax.ShapeDtypeStruct((CHIPS, QSTRIDE, PROJ), bf16),
        compiler_params=pltpu.CompilerParams(vmem_limit_bytes=58 * MIB),
        name="send_queries",
    )(page_ids, queries)


PROJ_ROWS = 2048
PROJ_SUB = 256
PROJ_STEPS = P_DEV * TOKP // PROJ_ROWS


def project_kernel(
    x_hbm, w_ref, emb_ref, scale_out, x_ref, value_ref, sems
):
    def part(step):
        return pl.ds(step * PROJ_ROWS, PROJ_ROWS)

    def load(step):
        return pltpu.make_async_copy(x_hbm.at[part(step)], x_ref.at[part(step)], sems.at[step])

    def normalize(at):
        rows = pl.ds(at, PROJ_SUB)
        value = value_ref[rows, :]
        scale = lax.rsqrt(jnp.sum(value * value, axis=1, keepdims=True) + epsilon)
        emb_ref[rows, :] = (value * scale).astype(bf16)
        for block in range(PROJ_SUB // 128):
            row = at // 128 + block
            scale_out[row : row + 1, :] = col_to_row(scale[block * 128 : block * 128 + 128], 128)

    for step in range(PROJ_STEPS):
        load(step).start()
    for step in range(PROJ_STEPS):
        load(step).wait()
        first = step * PROJ_ROWS
        for at in range(first, first + PROJ_ROWS, PROJ_SUB):
            value_ref[pl.ds(at, PROJ_SUB), :] = jnp.dot(
                x_ref[pl.ds(at, PROJ_SUB), :], w_ref[...], preferred_element_type=f32
            )
            if at > first:
                normalize(at - PROJ_SUB)
        normalize(first + PROJ_ROWS - PROJ_SUB)


def project(rows, weight):
    total = rows.shape[0]
    vmem = pl.BlockSpec(memory_space=pltpu.VMEM)
    hbm = pl.BlockSpec(memory_space=pltpu.HBM)
    return pl.pallas_call(
        project_kernel,
        in_specs=[hbm, vmem],
        out_specs=[vmem, vmem],
        out_shape=[
            jax.ShapeDtypeStruct((total, PROJ), bf16),
            jax.ShapeDtypeStruct((total // 128, 128), f32),
        ],
        scratch_shapes=[
            pltpu.VMEM((total, D_FEAT), bf16),
            pltpu.VMEM((total, PROJ), f32),
            pltpu.SemaphoreType.DMA((PROJ_STEPS,)),
        ],
        compiler_params=pltpu.CompilerParams(vmem_limit_bytes=36 * MIB),
        cost_estimate=pl.CostEstimate(
            flops=2 * total * D_FEAT * PROJ,
            bytes_accessed=total * (2 * D_FEAT + 2 * PROJ),
            transcendentals=0,
        ),
        name="project",
    )(rows, weight)


def receive(parts, recv_ref, sems):
    half = CHIPS * QSTRIDE
    copies = [
        pltpu.make_async_copy(part, recv_ref.at[pl.ds(i * half, half)], sems.at[i])
        for i, part in enumerate(parts)
    ]
    for copy in copies:
        copy.start()
    return copies


def slot_columns(recv_ref, core):
    meta = recv_ref[...].reshape(OWNERS, QSTRIDE, PROJ)[:, QROWS:QSTRIDE, :].astype(f32)
    meta = meta[:, 0:SLOTS, :].reshape(ENTRIES, PROJ)
    lane = iota((ENTRIES, PROJ), 1) - 2 * SLOTS * core
    slot = iota((ENTRIES, PROJ), 0) % SLOTS
    page = jnp.sum(jnp.where(lane == slot, meta, 0.0), axis=1, keepdims=True).astype(i32) - 1
    code = jnp.sum(jnp.where(lane == slot + SLOTS, meta, 0.0), axis=1, keepdims=True).astype(i32)
    source = iota((ENTRIES, 1), 0) // SLOTS
    other = source // CHIPS
    owner = 2 * (source % CHIPS) + jnp.where(other == 0, core, 1 - core)
    return page, owner * QBLOCK + code // 2, code // 2, code % 2


def plan_entries(page, of_source):
    valid = page >= 0
    page_f = page.astype(f32)
    page_row = col_to_row(page_f, ENTRIES)
    earlier = iota((ENTRIES, ENTRIES), 1) < iota((ENTRIES, ENTRIES), 0)
    rank = jnp.sum(
        jnp.where((page_f == page_row) & earlier, 1.0, 0.0), axis=1, keepdims=True
    )
    lane = iota((ENTRIES, 128), 1)
    on_page = (page == lane).astype(f32)
    count = jnp.sum(on_page, axis=0, keepdims=True)
    chunks = jnp.floor((count + (CHUNK - 1)) * (1.0 / CHUNK))
    upper = (iota((128, 128), 0) < iota((128, 128), 1)).astype(f32)
    start = jnp.dot(jnp.broadcast_to(chunks, (8, 128)), upper, preferred_element_type=f32)[0:1]
    position = jnp.sum(on_page * start, axis=1, keepdims=True) * CHUNK + rank
    position = jnp.where(valid, position, -1.0).astype(i32)
    at = position == iota((ENTRIES, POSITIONS), 1)
    entry_id = iota((ENTRIES, 1), 0)
    slot_row = jnp.sum(jnp.where(at, entry_id - ENTRIES, 0), axis=0, keepdims=True) + ENTRIES
    source = entry_id // SLOTS
    row_of = source * QSTRIDE + of_source * QTOK
    row_row = jnp.sum(jnp.where(at, row_of, 0), axis=0, keepdims=True)
    out_row = source * QROWS + of_source * QTOK
    query_row = jnp.sum(jnp.where(at, out_row, 0), axis=0, keepdims=True)
    start_col = row_to_col(start, 128)[0:P_DEV]
    chunk_page = (
        jnp.sum(
            jnp.where(start_col <= iota((P_DEV, 128), 1).astype(f32), 1, 0), axis=0, keepdims=True
        )
        - 1
    ) * TOKP
    total = jnp.sum(chunks, axis=1, keepdims=True).astype(i32)
    pad = jnp.zeros((1, POSITIONS - 256), i32)
    last = jnp.concatenate(
        [chunk_page, jnp.broadcast_to(total, (1, 128)), pad], axis=1
    )
    return jnp.concatenate(
        [slot_row, row_row, query_row, last, jnp.zeros((4, POSITIONS), i32)], axis=0
    )


def load_queries(recv_ref, table_ref, chunk):
    parts = []
    for j in range(CHUNK):
        row = pl.multiple_of(table_ref[1, chunk * CHUNK + j], 16)
        parts.append(recv_ref[pl.ds(row, QTOK), :])
    return jnp.concatenate(parts, axis=0)


def page_rows(table_ref, chunk):
    return pl.ds(pl.multiple_of(table_ref[3, chunk], TOKP), TOKP)


def chunk_sims(recv_ref, emb_ref, table_ref, chunk):
    return contract_last(
        emb_ref[page_rows(table_ref, chunk), :], load_queries(recv_ref, table_ref, chunk)
    )


def chunk_before(chunk, back):
    return jnp.where(chunk < back, EMPTY_CHUNK, chunk - back)


def forward_kernel(
    core_ref, own_any, other_any, emb_ref, back_ref, table_out, exps_ref,
    recv_ref, table_ref, logs_of, sims_ref, sems, recv_sems,
):
    core = core_ref[0]
    received = receive((own_any, other_any), recv_ref, recv_sems)
    sims_ref[...] = jnp.zeros(sims_ref.shape, f32)
    for copy in received:
        copy.wait()
    page, query, of_source, positive = slot_columns(recv_ref, core)
    table_out[...] = plan_entries(page, of_source)
    copy = pltpu.make_async_copy(table_out, table_ref, sems.at[0])
    copy.start()
    copy.wait()
    group = iota((1, 128), 1) // QTOK

    def steps(step, carry):
        for u in range(UNROLL):
            chunk = UNROLL * step + u
            sims_ref[u % 2] = chunk_sims(recv_ref, emb_ref, table_ref, chunk)
            chunk = chunk_before(chunk, 1)
            expw = jnp.exp2(sims_ref[(u + 1) % 2] * exp2_factor)
            logs = jnp.log2(jnp.sum(expw, axis=0, keepdims=True))
            for j in range(CHUNK):
                tile = logs[:, (j // 4) * 128 : (j // 4) * 128 + 128]
                slot = table_ref[0, chunk * CHUNK + j]
                logs_of[pl.ds(slot, 1), :] = jnp.where(group == j % 4, tile, 0.0)
        return carry

    lax.fori_loop(0, (table_ref[3, 128] + 1 + UNROLL - 1) // UNROLL, steps, 0)
    valid = page >= 0
    scores = log2_factor * jnp.sum(logs_of[0:ENTRIES, :], axis=1, keepdims=True)
    scores = jnp.where(valid, scores, 0.0)
    exps = jnp.where(valid, jnp.exp(scores), 0.0)
    exps_ref[...] = jnp.broadcast_to(exps, (ENTRIES, 128))
    lane = iota((ENTRIES, 128), 1)
    sums = jnp.sum(jnp.where(query == lane, exps, 0.0), axis=0, keepdims=True)
    slot = iota((ENTRIES, 128), 0) % SLOTS
    spread = jnp.where(lane == slot, scores, 0.0).reshape(OWNERS, SLOTS, 128)
    spread = jnp.sum(spread, axis=1, keepdims=True)
    which = iota((OWNERS, SLOTS, 128), 1)
    result = jnp.where(which == 0, sums[None], jnp.where(which == 1, spread, 0.0))
    own, other = result[0:CHIPS], result[CHIPS:OWNERS]
    back_ref[:, 0] = jnp.where(core == 0, own, other)
    back_ref[:, 1] = jnp.where(core == 0, other, own)


def forward(core, own, other, emb):
    vmem = pl.BlockSpec(memory_space=pltpu.VMEM)
    place = pl.BlockSpec(memory_space=pl.ANY)
    return pl.pallas_call(
        forward_kernel,
        in_specs=[
            pl.BlockSpec(memory_space=pltpu.SMEM),
            place,
            place,
            vmem,
        ],
        out_specs=[vmem, vmem, vmem],
        out_shape=[
            jax.ShapeDtypeStruct((CHIPS, 2, SLOTS, 128), f32),
            jax.ShapeDtypeStruct((8, POSITIONS), i32),
            jax.ShapeDtypeStruct((ENTRIES, 128), f32),
        ],
        scratch_shapes=[
            pltpu.VMEM((OWNERS * QSTRIDE, PROJ), bf16),
            pltpu.SMEM((8, POSITIONS), i32),
            pltpu.VMEM((ENTRIES + 8, 128), f32),
            pltpu.VMEM((2, TOKP, LANES), f32),
            pltpu.SemaphoreType.DMA((2,)),
            pltpu.SemaphoreType.DMA((2,)),
        ],
        compiler_params=pltpu.CompilerParams(vmem_limit_bytes=16 * MIB),
        name="forward",
    )(core, own, other, emb)


FEAT_STEPS = 5
FEAT_SUB = 1024
FEAT_ROWS = P_DEV * TOKP // FEAT_STEPS


def backward_kernel(
    core_ref, table_ref, exps_ref, sums_ref, scale_ref, own_any, other_any, emb_ref, feat_hbm,
    keep_ref, give_ref, recv_ref, weight_of, page_acc, query_acc, grad_ref, feat_ref, sims_ref, grads_ref, sems, recv_sems,
):
    def feature_copy(step):
        part = pl.ds(step * FEAT_ROWS, FEAT_ROWS)
        return pltpu.make_async_copy(feat_hbm.at[part], feat_ref.at[part], sems.at[step])

    received = receive((own_any, other_any), recv_ref, recv_sems)

    page_acc[...] = jnp.zeros(page_acc.shape, f32)
    query_acc[...] = jnp.zeros(query_acc.shape, f32)
    sims_ref[...] = jnp.zeros(sims_ref.shape, f32)
    grads_ref[...] = jnp.zeros(grads_ref.shape, bf16)
    for copy in received:
        copy.wait()
    page, query, of_source, positive = slot_columns(recv_ref, core_ref[0])
    sums = jnp.sum(sums_ref[...], axis=0)[0:1]
    lane = iota((ENTRIES, 128), 1)
    total = jnp.sum(jnp.where(query == lane, sums, 0.0), axis=1, keepdims=True)
    valid = page >= 0
    total = jnp.where(valid, total, 1.0)
    weight_of[0:ENTRIES, :] = jnp.where(
        valid, exps_ref[...] / total - positive.astype(f32), 0.0
    )
    weight_of[ENTRIES : ENTRIES + 8, :] = jnp.zeros((8, 128), f32)
    for step in range(FEAT_STEPS):
        feature_copy(step).start()
    group = iota((1, 128), 1) // QTOK

    def chunk_weights(chunk):
        tiles = []
        for half in range(CHUNK // 4):
            tile = jnp.zeros((1, 128), f32)
            for j in range(4):
                slot = table_ref[0, chunk * CHUNK + half * 4 + j]
                tile = jnp.where(group == j, weight_of[pl.ds(slot, 1), :], tile)
            tiles.append(tile)
        return jnp.concatenate(tiles, axis=1)

    def steps(step, carry):
        for u in range(UNROLL):
            chunk = UNROLL * step + u
            now, last = u % 2, (u + 1) % 2
            sims_ref[now] = chunk_sims(recv_ref, emb_ref, table_ref, chunk)

            middle = chunk_before(chunk, 1)
            expw = jnp.exp2(sims_ref[last] * exp2_factor)
            ratio = chunk_weights(middle) / jnp.sum(expw, axis=0, keepdims=True)
            grads_ref[last] = (expw * ratio).astype(bf16)

            oldest = chunk_before(chunk, 2)
            rows = page_rows(table_ref, oldest)
            sim_grad = grads_ref[now]
            page_part = jnp.dot(
                sim_grad, load_queries(recv_ref, table_ref, oldest), preferred_element_type=f32
            )
            query_part = contract_first(sim_grad, emb_ref[rows, :])
            page_acc[rows, :] += page_part
            for j in range(CHUNK):
                at = pl.ds(pl.multiple_of(table_ref[2, oldest * CHUNK + j], QTOK), QTOK)
                query_acc[at, :] += query_part[j * QTOK : (j + 1) * QTOK]
        return carry

    lax.fori_loop(0, (table_ref[3, 128] + 2 + UNROLL - 1) // UNROLL, steps, 0)
    half = CHIPS * QROWS
    for ref, at in ((keep_ref, 0), (give_ref, half)):
        ref[:, 0:QROWS, :] = query_acc[at : at + half, :].astype(bf16).reshape(CHIPS, QROWS, PROJ)

    def token_grads(at):
        for block in range(at // 128, (at + FEAT_SUB) // 128):
            part = pl.ds(block * 128, 128)
            unit = emb_ref[part, :].astype(f32)
            upstream = page_acc[part, :]
            scale = row_to_col(scale_ref[block : block + 1, :], 128)
            inner = jnp.sum(unit * upstream, axis=1, keepdims=True)
            grad_ref[part, :] = (scale * (upstream - unit * inner)).astype(bf16)

    total = P_DEV * TOKP
    grad = jnp.zeros((PROJ, D_FEAT), f32)
    token_grads(0)
    for at in range(0, total, FEAT_SUB):
        if at % FEAT_ROWS == 0:
            feature_copy(at // FEAT_ROWS).wait()
        if at + FEAT_SUB < total:
            token_grads(at + FEAT_SUB)
        part = pl.ds(at, FEAT_SUB)
        grad += contract_first(grad_ref[part, :], feat_ref[part, :])
    grad = grad.T
    pad = jnp.zeros((GRAD_PAD - GRAD_ROWS, PROJ), f32)
    first_core = core_ref[0] == 0
    for chip in range(CHIPS):
        at = 2 * chip * GRAD_ROWS
        even = jnp.concatenate([grad[at : at + GRAD_ROWS], pad], axis=0)
        odd = jnp.concatenate([grad[at + GRAD_ROWS : at + 2 * GRAD_ROWS], pad], axis=0)
        rows = pl.ds(QROWS, GRAD_PAD)
        keep_ref[chip, rows, :] = jnp.where(first_core, even, odd).astype(bf16)
        give_ref[chip, rows, :] = jnp.where(first_core, odd, even).astype(bf16)


def backward(core, table, exps, sums, scale, own, other, emb, rows):
    vmem = pl.BlockSpec(memory_space=pltpu.VMEM)
    hbm = pl.BlockSpec(memory_space=pltpu.HBM)
    smem = pl.BlockSpec(memory_space=pltpu.SMEM)
    place = pl.BlockSpec(memory_space=pl.ANY)
    return pl.pallas_call(
        backward_kernel,
        in_specs=[smem, smem, vmem, vmem, vmem, place, place, vmem, hbm],
        out_specs=[vmem, vmem],
        out_shape=[jax.ShapeDtypeStruct((CHIPS, QROWS + GRAD_PAD, PROJ), bf16)] * 2,
        scratch_shapes=[
            pltpu.VMEM((OWNERS * QSTRIDE, PROJ), bf16),
            pltpu.VMEM((ENTRIES + 8, 128), f32),
            pltpu.VMEM((P_DEV * TOKP, PROJ), f32),
            pltpu.VMEM((OWNERS * QROWS, PROJ), f32),
            pltpu.VMEM((P_DEV * TOKP, PROJ), bf16),
            pltpu.VMEM((P_DEV * TOKP, D_FEAT), bf16),
            pltpu.VMEM((2, TOKP, LANES), f32),
            pltpu.VMEM((2, TOKP, LANES), bf16),
            pltpu.SemaphoreType.DMA((FEAT_STEPS,)),
            pltpu.SemaphoreType.DMA((2,)),
        ],
        compiler_params=pltpu.CompilerParams(vmem_limit_bytes=40 * MIB),
        name="backward",
    )(core, table, exps, sums, scale, own, other, emb, rows)


def pair_sum(a, b):
    return (a.astype(f32) + b.astype(f32)).astype(bf16)


def share_kernel(parts_ref, out_ref):
    out_ref[...] = jnp.sum(parts_ref[:, QROWS : QROWS + GRAD_PAD, :].astype(f32), axis=0)


def own_share(parts):
    return pl.pallas_call(
        share_kernel,
        out_shape=jax.ShapeDtypeStruct((GRAD_PAD, PROJ), f32),
        compiler_params=SMALL,
        name="own_share",
    )(parts)


def spread_kernel(a_ref, b_ref, c_ref, d_ref, out_ref):
    total = (a_ref[...] + b_ref[...]) + (c_ref[...] + d_ref[...])
    out_ref[...] = jnp.broadcast_to(total.astype(bf16)[None], out_ref.shape)


def spread_share(shares):
    return pl.pallas_call(
        spread_kernel,
        out_shape=jax.ShapeDtypeStruct((OWNERS, GRAD_PAD, PROJ), bf16),
        compiler_params=SMALL,
        name="spread_share",
    )(*shares)


def collect_kernel(parts_ref, out_ref):
    for owner in range(OWNERS):
        rows = parts_ref[owner].astype(f32)[0:GRAD_ROWS]
        out_ref[owner * GRAD_ROWS : (owner + 1) * GRAD_ROWS, :] = rows


def collect(parts):
    return pl.pallas_call(
        collect_kernel,
        out_shape=jax.ShapeDtypeStruct((D_FEAT, PROJ), f32),
        compiler_params=SMALL,
        name="collect",
    )(parts)


def query_kernel(parts_ref, q_ref, out_ref):
    upstream = jnp.sum(parts_ref[:, 0:QROWS, :].astype(f32), axis=0)
    wide = q_ref[...].reshape(QROWS, PROJ).astype(f32)
    scale = lax.rsqrt(jnp.sum(wide * wide, axis=1, keepdims=True) + epsilon)
    inner = jnp.sum(wide * upstream, axis=1, keepdims=True)
    out_ref[...] = (upstream * scale - wide * (scale * scale * scale * inner)).reshape(
        out_ref.shape
    )


def query_grads(parts, queries):
    return pl.pallas_call(
        query_kernel,
        out_shape=jax.ShapeDtypeStruct(queries.shape, f32),
        compiler_params=SMALL,
        name="query_grads",
    )(parts, queries)


def listed_scores(sums, page_ids):
    owner_of = page_ids.reshape(-1) // P_DEV
    hits = (owner_of[:, None] == jnp.arange(OWNERS, dtype=i32)[None, :]).astype(i32)
    rank_of = jnp.sum(jnp.cumsum(hits, axis=0) * hits, axis=1) - 1
    slots = sums[:, 1, 0:SLOTS]
    pick = (hits != 0)[:, :, None] & (rank_of[:, None] == jnp.arange(SLOTS, dtype=i32))[:, None, :]
    return jnp.sum(jnp.where(pick, slots[None], 0.0), axis=(1, 2)).reshape(page_ids.shape)


def exchange(values, axes, groups=None):
    return lax.all_to_all(
        values, axes, split_axis=0, concat_axis=0, axis_index_groups=groups, tiled=True
    )


def per_device(features, queries, proj_weight, page_ids):
    rows = features.reshape(P_DEV * TOKP, D_FEAT)
    same_core = [list(range(first, OWNERS, 2)) for first in range(2)]
    other_core = [(i, i ^ 1) for i in range(OWNERS)]
    core = (lax.axis_index("pages") % 2).astype(i32).reshape(1)
    own = exchange(send_queries(page_ids, queries), "pages", same_core)
    own, emb, scale = lax.optimization_barrier((own, *project(rows, proj_weight)))
    other = lax.ppermute(own, "pages", other_core)
    own = own.reshape(CHIPS * QSTRIDE, PROJ)
    other = other.reshape(CHIPS * QSTRIDE, PROJ)
    back, table, exps = forward(core, own, other, emb)
    sums = exchange(back.reshape(OWNERS, SLOTS, 128), "pages")
    keep, give = backward(core, table, exps, sums, scale, own, other, emb, rows)
    taken = lax.ppermute(give, "pages", other_core)
    parts = exchange(pair_sum(keep, taken), "pages", same_core)
    share = own_share(parts)
    replicas = lax.axis_size("rep")
    shares = [share] + [
        lax.ppermute(share, "rep", [(i, i ^ k) for i in range(replicas)]) for k in (1, 2, 3)
    ]
    grad_proj = collect(exchange(spread_share(shares), "pages"))
    grad_query = query_grads(parts, queries)
    scores = listed_scores(sums, page_ids)
    return (scores, grad_query, grad_proj)


def solution(mesh):
    in_specs = (
        P("pages", None, None),
        P(("pages", "rep"), None, None),
        P(),
        P(("pages", "rep"), None),
    )
    out_specs = (P(("pages", "rep"), None), P(("pages", "rep"), None, None), P())
    return jax.shard_map(
        per_device, mesh=mesh, in_specs=in_specs, out_specs=out_specs, check_vma=False
    )
```

```python
import math

import jax
import jax.numpy as jnp
from jax import lax
from jax.experimental import pallas as pl
from jax.experimental.pallas import tpu as pltpu
from jax.sharding import PartitionSpec as P

epsilon = 1e-06
smoothing = 0.05
exp2_factor = 1.0 / (smoothing * math.log(2.0))
log2_factor = smoothing * math.log(2.0)

f32 = jnp.float32
bf16 = jnp.bfloat16
i32 = jnp.int32

OWNERS = 32
SLOTS = 8
ENTRIES = OWNERS * SLOTS
QBLOCK = 4
LISTED = 16
QTOK = 32
TOKP = 256
PROJ = 128
P_DEV = 40
D_FEAT = 1152
META = 16
QROWS = QBLOCK * QTOK
QSTRIDE = QROWS + META
CHUNK = 8
LANES = CHUNK * QTOK
GRAD_ROWS = D_FEAT // OWNERS
GRAD_PAD = 48
CHIPS = OWNERS // 2
POSITIONS = 640
EMPTY_CHUNK = POSITIONS // CHUNK - 1
UNROLL = 6
MIB = 1 << 20
SMALL = pltpu.CompilerParams(vmem_limit_bytes=8 * MIB)


def iota(shape, dim):
    return lax.broadcasted_iota(i32, shape, dim)


def row_to_col(row, n):
    same = iota((n, n), 0) == iota((n, n), 1)
    return jnp.sum(jnp.where(same, jnp.broadcast_to(row, (n, n)), 0.0), axis=1, keepdims=True)


def col_to_row(col, n):
    same = iota((n, n), 0) == iota((n, n), 1)
    return jnp.sum(jnp.where(same, jnp.broadcast_to(col, (n, n)), 0.0), axis=0, keepdims=True)


def contract_first(a, b):
    return lax.dot_general(a, b, (((0,), (0,)), ((), ())), preferred_element_type=f32)


def contract_last(a, b):
    return lax.dot_general(a, b, (((1,), (1,)), ((), ())), preferred_element_type=f32)


def send_kernel(ids_ref, q_ref, out_ref):
    wide = q_ref[...].reshape(QROWS, PROJ).astype(f32)
    scale = lax.rsqrt(jnp.sum(wide * wide, axis=1, keepdims=True) + epsilon)
    emb = (wide * scale).astype(bf16)
    out_ref[:, 0:QROWS, :] = jnp.broadcast_to(emb[None], (CHIPS, QROWS, PROJ))
    ids = ids_ref[...].astype(f32)
    owner = jnp.floor((ids + 0.5) * (1.0 / P_DEV))
    local = ids - owner * P_DEV
    owner_col = jnp.concatenate([row_to_col(owner[q : q + 1], LISTED) for q in range(QBLOCK)], 0)
    local_col = jnp.concatenate([row_to_col(local[q : q + 1], LISTED) for q in range(QBLOCK)], 0)
    pairs = QBLOCK * LISTED
    lane = iota((pairs, 128), 1)
    entry = iota((pairs, 128), 0)
    hit = (owner_col.astype(i32) == lane).astype(f32)
    before = (iota((pairs, pairs), 1) < iota((pairs, pairs), 0)).astype(f32)
    rank = jnp.sum(
        hit * jnp.dot(before, hit, preferred_element_type=f32), axis=1, keepdims=True
    ).astype(i32)
    code = (entry // LISTED) * 2 + (entry % LISTED == 0).astype(i32)
    base = rank + 2 * SLOTS * (owner_col.astype(i32) % 2)
    value = jnp.where(
        base == lane,
        local_col + 1.0,
        jnp.where(base + SLOTS == lane, code.astype(f32), 0.0),
    )
    on_chip = (owner_col.astype(i32) // 2 == lane).astype(f32)
    meta = contract_first(on_chip, value)[0:CHIPS]
    out_ref[:, QROWS:QSTRIDE, :] = jnp.broadcast_to(
        meta[:, None, :], (CHIPS, META, PROJ)
    ).astype(bf16)


def send_queries(page_ids, queries):
    return pl.pallas_call(
        send_kernel,
        out_shape=jax.ShapeDtypeStruct((CHIPS, QSTRIDE, PROJ), bf16),
        compiler_params=pltpu.CompilerParams(vmem_limit_bytes=58 * MIB),
        name="send_queries",
    )(page_ids, queries)


PROJ_ROWS = 2048
PROJ_SUB = 256
PROJ_STEPS = P_DEV * TOKP // PROJ_ROWS


def project_kernel(
    x_hbm, w_ref, emb_ref, scale_out, x_ref, value_ref, sems
):
    def part(step):
        return pl.ds(step * PROJ_ROWS, PROJ_ROWS)

    def load(step):
        return pltpu.make_async_copy(x_hbm.at[part(step)], x_ref.at[part(step)], sems.at[step])

    def normalize(at):
        rows = pl.ds(at, PROJ_SUB)
        value = value_ref[rows, :]
        scale = lax.rsqrt(jnp.sum(value * value, axis=1, keepdims=True) + epsilon)
        emb_ref[rows, :] = (value * scale).astype(bf16)
        for block in range(PROJ_SUB // 128):
            row = at // 128 + block
            scale_out[row : row + 1, :] = col_to_row(scale[block * 128 : block * 128 + 128], 128)

    for step in range(PROJ_STEPS):
        load(step).start()
    for step in range(PROJ_STEPS):
        load(step).wait()
        first = step * PROJ_ROWS
        for at in range(first, first + PROJ_ROWS, PROJ_SUB):
            value_ref[pl.ds(at, PROJ_SUB), :] = jnp.dot(
                x_ref[pl.ds(at, PROJ_SUB), :], w_ref[...], preferred_element_type=f32
            )
            if at > first:
                normalize(at - PROJ_SUB)
        normalize(first + PROJ_ROWS - PROJ_SUB)


def project(rows, weight):
    total = rows.shape[0]
    vmem = pl.BlockSpec(memory_space=pltpu.VMEM)
    hbm = pl.BlockSpec(memory_space=pltpu.HBM)
    return pl.pallas_call(
        project_kernel,
        in_specs=[hbm, vmem],
        out_specs=[vmem, vmem],
        out_shape=[
            jax.ShapeDtypeStruct((total, PROJ), bf16),
            jax.ShapeDtypeStruct((total // 128, 128), f32),
        ],
        scratch_shapes=[
            pltpu.VMEM((total, D_FEAT), bf16),
            pltpu.VMEM((total, PROJ), f32),
            pltpu.SemaphoreType.DMA((PROJ_STEPS,)),
        ],
        compiler_params=pltpu.CompilerParams(vmem_limit_bytes=36 * MIB),
        cost_estimate=pl.CostEstimate(
            flops=2 * total * D_FEAT * PROJ,
            bytes_accessed=total * (2 * D_FEAT + 2 * PROJ),
            transcendentals=0,
        ),
        name="project",
    )(rows, weight)


def receive(parts, recv_ref, sems):
    half = CHIPS * QSTRIDE
    copies = [
        pltpu.make_async_copy(part, recv_ref.at[pl.ds(i * half, half)], sems.at[i])
        for i, part in enumerate(parts)
    ]
    for copy in copies:
        copy.start()
    return copies


def slot_columns(recv_ref, core):
    meta = recv_ref[...].reshape(OWNERS, QSTRIDE, PROJ)[:, QROWS:QSTRIDE, :].astype(f32)
    meta = meta[:, 0:SLOTS, :].reshape(ENTRIES, PROJ)
    lane = iota((ENTRIES, PROJ), 1) - 2 * SLOTS * core
    slot = iota((ENTRIES, PROJ), 0) % SLOTS
    page = jnp.sum(jnp.where(lane == slot, meta, 0.0), axis=1, keepdims=True).astype(i32) - 1
    code = jnp.sum(jnp.where(lane == slot + SLOTS, meta, 0.0), axis=1, keepdims=True).astype(i32)
    source = iota((ENTRIES, 1), 0) // SLOTS
    other = source // CHIPS
    owner = 2 * (source % CHIPS) + jnp.where(other == 0, core, 1 - core)
    return page, owner * QBLOCK + code // 2, code // 2, code % 2


def plan_entries(page, of_source):
    valid = page >= 0
    page_f = page.astype(f32)
    page_row = col_to_row(page_f, ENTRIES)
    earlier = iota((ENTRIES, ENTRIES), 1) < iota((ENTRIES, ENTRIES), 0)
    rank = jnp.sum(
        jnp.where((page_f == page_row) & earlier, 1.0, 0.0), axis=1, keepdims=True
    )
    lane = iota((ENTRIES, 128), 1)
    on_page = (page == lane).astype(f32)
    count = jnp.sum(on_page, axis=0, keepdims=True)
    chunks = jnp.floor((count + (CHUNK - 1)) * (1.0 / CHUNK))
    upper = (iota((128, 128), 0) < iota((128, 128), 1)).astype(f32)
    start = jnp.dot(jnp.broadcast_to(chunks, (8, 128)), upper, preferred_element_type=f32)[0:1]
    position = jnp.sum(on_page * start, axis=1, keepdims=True) * CHUNK + rank
    position = jnp.where(valid, position, -1.0).astype(i32)
    at = position == iota((ENTRIES, POSITIONS), 1)
    entry_id = iota((ENTRIES, 1), 0)
    slot_row = jnp.sum(jnp.where(at, entry_id - ENTRIES, 0), axis=0, keepdims=True) + ENTRIES
    source = entry_id // SLOTS
    row_of = source * QSTRIDE + of_source * QTOK
    row_row = jnp.sum(jnp.where(at, row_of, 0), axis=0, keepdims=True)
    out_row = source * QROWS + of_source * QTOK
    query_row = jnp.sum(jnp.where(at, out_row, 0), axis=0, keepdims=True)
    start_col = row_to_col(start, 128)[0:P_DEV]
    chunk_page = (
        jnp.sum(
            jnp.where(start_col <= iota((P_DEV, 128), 1).astype(f32), 1, 0), axis=0, keepdims=True
        )
        - 1
    ) * TOKP
    total = jnp.sum(chunks, axis=1, keepdims=True).astype(i32)
    pad = jnp.zeros((1, POSITIONS - 256), i32)
    last = jnp.concatenate(
        [chunk_page, jnp.broadcast_to(total, (1, 128)), pad], axis=1
    )
    return jnp.concatenate(
        [slot_row, row_row, query_row, last, jnp.zeros((4, POSITIONS), i32)], axis=0
    )


def load_queries(recv_ref, table_ref, chunk):
    parts = []
    for j in range(CHUNK):
        row = pl.multiple_of(table_ref[1, chunk * CHUNK + j], 16)
        parts.append(recv_ref[pl.ds(row, QTOK), :])
    return jnp.concatenate(parts, axis=0)


def page_rows(table_ref, chunk):
    return pl.ds(pl.multiple_of(table_ref[3, chunk], TOKP), TOKP)


def chunk_sims(recv_ref, emb_ref, table_ref, chunk):
    return contract_last(
        emb_ref[page_rows(table_ref, chunk), :], load_queries(recv_ref, table_ref, chunk)
    )


def chunk_before(chunk, back):
    return jnp.where(chunk < back, EMPTY_CHUNK, chunk - back)


def forward_kernel(
    core_ref, own_any, other_any, emb_ref, back_ref, table_out, exps_ref,
    recv_ref, table_ref, logs_of, sims_ref, sems, recv_sems,
):
    core = core_ref[0]
    received = receive((own_any, other_any), recv_ref, recv_sems)
    sims_ref[...] = jnp.zeros(sims_ref.shape, f32)
    for copy in received:
        copy.wait()
    page, query, of_source, positive = slot_columns(recv_ref, core)
    table_out[...] = plan_entries(page, of_source)
    copy = pltpu.make_async_copy(table_out, table_ref, sems.at[0])
    copy.start()
    copy.wait()
    group = iota((1, 128), 1) // QTOK

    def steps(step, carry):
        for u in range(UNROLL):
            chunk = UNROLL * step + u
            sims_ref[u % 2] = chunk_sims(recv_ref, emb_ref, table_ref, chunk)
            chunk = chunk_before(chunk, 1)
            expw = jnp.exp2(sims_ref[(u + 1) % 2] * exp2_factor)
            logs = jnp.log2(jnp.sum(expw, axis=0, keepdims=True))
            for j in range(CHUNK):
                tile = logs[:, (j // 4) * 128 : (j // 4) * 128 + 128]
                slot = table_ref[0, chunk * CHUNK + j]
                logs_of[pl.ds(slot, 1), :] = jnp.where(group == j % 4, tile, 0.0)
        return carry

    lax.fori_loop(0, (table_ref[3, 128] + 1 + UNROLL - 1) // UNROLL, steps, 0)
    valid = page >= 0
    scores = log2_factor * jnp.sum(logs_of[0:ENTRIES, :], axis=1, keepdims=True)
    scores = jnp.where(valid, scores, 0.0)
    exps = jnp.where(valid, jnp.exp(scores), 0.0)
    exps_ref[...] = jnp.broadcast_to(exps, (ENTRIES, 128))
    lane = iota((ENTRIES, 128), 1)
    sums = jnp.sum(jnp.where(query == lane, exps, 0.0), axis=0, keepdims=True)
    slot = iota((ENTRIES, 128), 0) % SLOTS
    spread = jnp.where(lane == slot, scores, 0.0).reshape(OWNERS, SLOTS, 128)
    spread = jnp.sum(spread, axis=1, keepdims=True)
    which = iota((OWNERS, SLOTS, 128), 1)
    result = jnp.where(which == 0, sums[None], jnp.where(which == 1, spread, 0.0))
    own, other = result[0:CHIPS], result[CHIPS:OWNERS]
    back_ref[:, 0] = jnp.where(core == 0, own, other)
    back_ref[:, 1] = jnp.where(core == 0, other, own)


def forward(core, own, other, emb):
    vmem = pl.BlockSpec(memory_space=pltpu.VMEM)
    place = pl.BlockSpec(memory_space=pl.ANY)
    return pl.pallas_call(
        forward_kernel,
        in_specs=[
            pl.BlockSpec(memory_space=pltpu.SMEM),
            place,
            place,
            vmem,
        ],
        out_specs=[vmem, vmem, vmem],
        out_shape=[
            jax.ShapeDtypeStruct((CHIPS, 2, SLOTS, 128), f32),
            jax.ShapeDtypeStruct((8, POSITIONS), i32),
            jax.ShapeDtypeStruct((ENTRIES, 128), f32),
        ],
        scratch_shapes=[
            pltpu.VMEM((OWNERS * QSTRIDE, PROJ), bf16),
            pltpu.SMEM((8, POSITIONS), i32),
            pltpu.VMEM((ENTRIES + 8, 128), f32),
            pltpu.VMEM((2, TOKP, LANES), f32),
            pltpu.SemaphoreType.DMA((2,)),
            pltpu.SemaphoreType.DMA((2,)),
        ],
        compiler_params=pltpu.CompilerParams(vmem_limit_bytes=16 * MIB),
        name="forward",
    )(core, own, other, emb)


FEAT_STEPS = 5
FEAT_SUB = 512
FEAT_ROWS = P_DEV * TOKP // FEAT_STEPS


def backward_kernel(
    core_ref, table_ref, exps_ref, sums_ref, scale_ref, own_any, other_any, emb_ref, feat_hbm,
    keep_ref, give_ref, recv_ref, weight_of, page_acc, query_acc, grad_ref, feat_ref, sims_ref, grads_ref, sems, recv_sems,
):
    def feature_copy(step):
        part = pl.ds(step * FEAT_ROWS, FEAT_ROWS)
        return pltpu.make_async_copy(feat_hbm.at[part], feat_ref.at[part], sems.at[step])

    received = receive((own_any, other_any), recv_ref, recv_sems)

    page_acc[...] = jnp.zeros(page_acc.shape, f32)
    query_acc[...] = jnp.zeros(query_acc.shape, f32)
    sims_ref[...] = jnp.zeros(sims_ref.shape, f32)
    grads_ref[...] = jnp.zeros(grads_ref.shape, bf16)
    for copy in received:
        copy.wait()
    for step in range(FEAT_STEPS):
        feature_copy(step).start()
    page, query, of_source, positive = slot_columns(recv_ref, core_ref[0])
    sums = jnp.sum(sums_ref[...], axis=0)[0:1]
    lane = iota((ENTRIES, 128), 1)
    total = jnp.sum(jnp.where(query == lane, sums, 0.0), axis=1, keepdims=True)
    valid = page >= 0
    total = jnp.where(valid, total, 1.0)
    weight_of[0:ENTRIES, :] = jnp.where(
        valid, exps_ref[...] / total - positive.astype(f32), 0.0
    )
    weight_of[ENTRIES : ENTRIES + 8, :] = jnp.zeros((8, 128), f32)
    group = iota((1, 128), 1) // QTOK

    def chunk_weights(chunk):
        tiles = []
        for half in range(CHUNK // 4):
            tile = jnp.zeros((1, 128), f32)
            for j in range(4):
                slot = table_ref[0, chunk * CHUNK + half * 4 + j]
                tile = jnp.where(group == j, weight_of[pl.ds(slot, 1), :], tile)
            tiles.append(tile)
        return jnp.concatenate(tiles, axis=1)

    def steps(step, carry):
        for u in range(UNROLL):
            chunk = UNROLL * step + u
            now, last = u % 2, (u + 1) % 2
            sims_ref[now] = chunk_sims(recv_ref, emb_ref, table_ref, chunk)

            middle = chunk_before(chunk, 1)
            expw = jnp.exp2(sims_ref[last] * exp2_factor)
            ratio = chunk_weights(middle) / jnp.sum(expw, axis=0, keepdims=True)
            grads_ref[last] = (expw * ratio).astype(bf16)

            oldest = chunk_before(chunk, 2)
            rows = page_rows(table_ref, oldest)
            sim_grad = grads_ref[now]
            page_part = jnp.dot(
                sim_grad, load_queries(recv_ref, table_ref, oldest), preferred_element_type=f32
            )
            query_part = contract_first(sim_grad, emb_ref[rows, :])
            page_acc[rows, :] += page_part
            for j in range(CHUNK):
                at = pl.ds(pl.multiple_of(table_ref[2, oldest * CHUNK + j], QTOK), QTOK)
                query_acc[at, :] += query_part[j * QTOK : (j + 1) * QTOK]
        return carry

    lax.fori_loop(0, (table_ref[3, 128] + 2 + UNROLL - 1) // UNROLL, steps, 0)
    half = CHIPS * QROWS
    for ref, at in ((keep_ref, 0), (give_ref, half)):
        ref[:, 0:QROWS, :] = query_acc[at : at + half, :].astype(bf16).reshape(CHIPS, QROWS, PROJ)

    def token_grads(at):
        for block in range(at // 128, (at + FEAT_SUB) // 128):
            part = pl.ds(block * 128, 128)
            unit = emb_ref[part, :].astype(f32)
            upstream = page_acc[part, :]
            scale = row_to_col(scale_ref[block : block + 1, :], 128)
            inner = jnp.sum(unit * upstream, axis=1, keepdims=True)
            grad_ref[part, :] = (scale * (upstream - unit * inner)).astype(bf16)

    total = P_DEV * TOKP
    grad = jnp.zeros((PROJ, D_FEAT), f32)
    token_grads(0)
    for at in range(0, total, FEAT_SUB):
        if at % FEAT_ROWS == 0:
            feature_copy(at // FEAT_ROWS).wait()
        if at + FEAT_SUB < total:
            token_grads(at + FEAT_SUB)
        part = pl.ds(at, FEAT_SUB)
        grad += contract_first(grad_ref[part, :], feat_ref[part, :])
    grad = grad.T
    pad = jnp.zeros((GRAD_PAD - GRAD_ROWS, PROJ), f32)
    first_core = core_ref[0] == 0
    for chip in range(CHIPS):
        at = 2 * chip * GRAD_ROWS
        even = jnp.concatenate([grad[at : at + GRAD_ROWS], pad], axis=0)
        odd = jnp.concatenate([grad[at + GRAD_ROWS : at + 2 * GRAD_ROWS], pad], axis=0)
        rows = pl.ds(QROWS, GRAD_PAD)
        keep_ref[chip, rows, :] = jnp.where(first_core, even, odd).astype(bf16)
        give_ref[chip, rows, :] = jnp.where(first_core, odd, even).astype(bf16)


def backward(core, table, exps, sums, scale, own, other, emb, rows):
    vmem = pl.BlockSpec(memory_space=pltpu.VMEM)
    hbm = pl.BlockSpec(memory_space=pltpu.HBM)
    smem = pl.BlockSpec(memory_space=pltpu.SMEM)
    place = pl.BlockSpec(memory_space=pl.ANY)
    return pl.pallas_call(
        backward_kernel,
        in_specs=[smem, smem, vmem, vmem, vmem, place, place, vmem, hbm],
        out_specs=[vmem, vmem],
        out_shape=[jax.ShapeDtypeStruct((CHIPS, QROWS + GRAD_PAD, PROJ), bf16)] * 2,
        scratch_shapes=[
            pltpu.VMEM((OWNERS * QSTRIDE, PROJ), bf16),
            pltpu.VMEM((ENTRIES + 8, 128), f32),
            pltpu.VMEM((P_DEV * TOKP, PROJ), f32),
            pltpu.VMEM((OWNERS * QROWS, PROJ), f32),
            pltpu.VMEM((P_DEV * TOKP, PROJ), bf16),
            pltpu.VMEM((P_DEV * TOKP, D_FEAT), bf16),
            pltpu.VMEM((2, TOKP, LANES), f32),
            pltpu.VMEM((2, TOKP, LANES), bf16),
            pltpu.SemaphoreType.DMA((FEAT_STEPS,)),
            pltpu.SemaphoreType.DMA((2,)),
        ],
        compiler_params=pltpu.CompilerParams(vmem_limit_bytes=40 * MIB),
        name="backward",
    )(core, table, exps, sums, scale, own, other, emb, rows)


def pair_sum(a, b):
    return (a.astype(f32) + b.astype(f32)).astype(bf16)


def share_kernel(parts_ref, out_ref):
    out_ref[...] = jnp.sum(parts_ref[:, QROWS : QROWS + GRAD_PAD, :].astype(f32), axis=0)


def own_share(parts):
    return pl.pallas_call(
        share_kernel,
        out_shape=jax.ShapeDtypeStruct((GRAD_PAD, PROJ), f32),
        compiler_params=SMALL,
        name="own_share",
    )(parts)


def spread_kernel(a_ref, b_ref, c_ref, d_ref, out_ref):
    total = (a_ref[...] + b_ref[...]) + (c_ref[...] + d_ref[...])
    out_ref[...] = jnp.broadcast_to(total.astype(bf16)[None], out_ref.shape)


def spread_share(shares):
    return pl.pallas_call(
        spread_kernel,
        out_shape=jax.ShapeDtypeStruct((OWNERS, GRAD_PAD, PROJ), bf16),
        compiler_params=SMALL,
        name="spread_share",
    )(*shares)


def collect_kernel(parts_ref, out_ref):
    for owner in range(OWNERS):
        rows = parts_ref[owner].astype(f32)[0:GRAD_ROWS]
        out_ref[owner * GRAD_ROWS : (owner + 1) * GRAD_ROWS, :] = rows


def collect(parts):
    return pl.pallas_call(
        collect_kernel,
        out_shape=jax.ShapeDtypeStruct((D_FEAT, PROJ), f32),
        compiler_params=SMALL,
        name="collect",
    )(parts)


def query_kernel(parts_ref, q_ref, out_ref):
    upstream = jnp.sum(parts_ref[:, 0:QROWS, :].astype(f32), axis=0)
    wide = q_ref[...].reshape(QROWS, PROJ).astype(f32)
    scale = lax.rsqrt(jnp.sum(wide * wide, axis=1, keepdims=True) + epsilon)
    inner = jnp.sum(wide * upstream, axis=1, keepdims=True)
    out_ref[...] = (upstream * scale - wide * (scale * scale * scale * inner)).reshape(
        out_ref.shape
    )


def query_grads(parts, queries):
    return pl.pallas_call(
        query_kernel,
        out_shape=jax.ShapeDtypeStruct(queries.shape, f32),
        compiler_params=SMALL,
        name="query_grads",
    )(parts, queries)


def listed_scores(sums, page_ids):
    owner_of = page_ids.reshape(-1) // P_DEV
    hits = (owner_of[:, None] == jnp.arange(OWNERS, dtype=i32)[None, :]).astype(i32)
    rank_of = jnp.sum(jnp.cumsum(hits, axis=0) * hits, axis=1) - 1
    slots = sums[:, 1, 0:SLOTS]
    pick = (hits != 0)[:, :, None] & (rank_of[:, None] == jnp.arange(SLOTS, dtype=i32))[:, None, :]
    return jnp.sum(jnp.where(pick, slots[None], 0.0), axis=(1, 2)).reshape(page_ids.shape)


def exchange(values, axes, groups=None):
    return lax.all_to_all(
        values, axes, split_axis=0, concat_axis=0, axis_index_groups=groups, tiled=True
    )


def per_device(features, queries, proj_weight, page_ids):
    rows = features.reshape(P_DEV * TOKP, D_FEAT)
    same_core = [list(range(first, OWNERS, 2)) for first in range(2)]
    other_core = [(i, i ^ 1) for i in range(OWNERS)]
    core = (lax.axis_index("pages") % 2).astype(i32).reshape(1)
    own = exchange(send_queries(page_ids, queries), "pages", same_core)
    own, emb, scale = lax.optimization_barrier((own, *project(rows, proj_weight)))
    other = lax.ppermute(own, "pages", other_core)
    own = own.reshape(CHIPS * QSTRIDE, PROJ)
    other = other.reshape(CHIPS * QSTRIDE, PROJ)
    back, table, exps = forward(core, own, other, emb)
    sums = exchange(back.reshape(OWNERS, SLOTS, 128), "pages")
    keep, give = backward(core, table, exps, sums, scale, own, other, emb, rows)
    taken = lax.ppermute(give, "pages", other_core)
    parts = exchange(pair_sum(keep, taken), "pages", same_core)
    share = own_share(parts)
    replicas = lax.axis_size("rep")
    shares = [share] + [
        lax.ppermute(share, "rep", [(i, i ^ k) for i in range(replicas)]) for k in (1, 2, 3)
    ]
    grad_proj = collect(exchange(spread_share(shares), "pages"))
    grad_query = query_grads(parts, queries)
    scores = listed_scores(sums, page_ids)
    return (scores, grad_query, grad_proj)


def solution(mesh):
    in_specs = (
        P("pages", None, None),
        P(("pages", "rep"), None, None),
        P(),
        P(("pages", "rep"), None),
    )
    out_specs = (P(("pages", "rep"), None), P(("pages", "rep"), None, None), P())
    return jax.shard_map(
        per_device, mesh=mesh, in_specs=in_specs, out_specs=out_specs, check_vma=False
    )
```
